512 devices in a mesh: seq: 64 (over y, z_lo, core), ch: 8 (over x, z_hi).
Axes of the slice: x: 4, y: 4, z: 16 (z_hi: 2, z_lo: 8; z = z_hi * 8 + z_lo), core: 2. Of those that a mesh axis runs over, the one named last changes fastest.
Arguments:
- query: bfloat16 [16384, 2048], P('seq', 'ch'), may hold values from -6 to 6
- key_proj: bfloat16 [16384, 2048], P('seq', 'ch'), may hold values from -6 to 6
- value: bfloat16 [16384, 2048], P('seq', 'ch'), may hold values from -6 to 6
- filt: float32 [16384, 2048], P('seq', 'ch'), may hold values from -0.046875 to 0.046875
- skip: float32 [2048], P('ch'), may hold values from 0.5 to 1.5
- cotangent: bfloat16 [16384, 2048], P('seq', 'ch'), may hold values from -6 to 6
- suffix_start: int32 [1], replicated, may hold values from 4096 to 8191
- layer_input: bfloat16 [16384, 2048], P('seq', 'ch'), may hold values from -2 to 2
- in_weight: bfloat16 [6144, 2048], P(None, 'ch'), may hold values from -0.078125 to 0.078125
Outputs:
- input_grad: bfloat16 [16384, 2048], P('seq', 'ch')
- attribution: float32 [16384], P('seq')
The draws below stay inside these ranges and needn't reach their ends.
All inputs are finite; a program needn't handle non-finite values.
Results may differ from the reference program's by a relative error of at most 0.0049.
Values may be sent and summed in bfloat16 or wider, within the bound.
A program may use at most 64 MiB of HBM per device.

```python
import jax
import jax.numpy as jnp
from jax import lax

D = 2048
CH = 2048
SEQ = 16384


def shard_levels(key, extent, pieces, smallest, largest):
    gain = 1.0
    for dim, blocks in pieces:
        heights = jax.random.uniform(jax.random.fold_in(jax.random.fold_in(key, 6), dim), (blocks,), jnp.float32, smallest / len(pieces), largest / len(pieces))
        gain = gain * jnp.repeat(jnp.exp(heights), extent[dim] // blocks).reshape((-1,) + (1,) * (len(extent) - 1 - dim))
    return gain


def centred(stream_key, extent, spread, reach, pieces=(), kind=jnp.bfloat16):
    values = jax.random.normal(stream_key, extent, jnp.float32) * spread
    if len(pieces) > 0:
        values = shard_levels(stream_key, extent, pieces, -0.22, 0.18) * values
    return jnp.clip(values, min=-reach, max=reach).astype(kind)


def setup_inputs(seed: int = 0) -> dict:
    streams_of = jax.random.split(jax.random.key(seed), 10)
    query = centred(streams_of[0], (SEQ, CH), 1.0, 6.0, ((0, 64), (1, 8)))
    key_proj = centred(streams_of[1], (SEQ, CH), 1.0, 6.0, ((0, 64), (1, 8)))
    value = centred(streams_of[2], (SEQ, CH), 1.0, 6.0, ((0, 64), (1, 8)))
    filt = centred(streams_of[3], (SEQ, CH), SEQ ** -0.5, 0.046875, ((0, 64), (1, 8)), jnp.float32)
    skip = jnp.clip(0.5 + 1.0 * jax.random.uniform(streams_of[4], (CH,), jnp.float32) ** shard_levels(streams_of[4], (CH,), ((0, 8),), -0.2, 0.2), 0.5, 1.5)
    cotangent = centred(streams_of[5], (SEQ, CH), 1.0, 6.0, ((0, 64), (1, 8)))
    suffix_start = jax.random.randint(streams_of[6], (1,), SEQ // 4, SEQ // 2).astype(jnp.int32)
    layer_input = centred(streams_of[7], (SEQ, D), 0.125, 2.0, ((0, 64), (1, 8)))
    in_weight = centred(streams_of[8], (3 * CH, D), (3 * CH) ** -0.5, 0.078125, ((1, 8),))
    return dict(query=query, key_proj=key_proj, value=value, filt=filt, skip=skip, cotangent=cotangent, suffix_start=suffix_start, layer_input=layer_input, in_weight=in_weight)


def convolve_pair(triple):
    mixed, grad_mixed_in, filt = triple
    length = mixed.shape[0]
    total = 2 * length
    filt_spec = jnp.fft.rfft(filt, n=total, axis=0)
    conv_out = jnp.fft.irfft(filt_spec * jnp.fft.rfft(mixed, n=total, axis=0), n=total, axis=0)[:length]
    corr_out = jnp.fft.irfft(jnp.conj(filt_spec) * jnp.fft.rfft(grad_mixed_in, n=total, axis=0), n=total, axis=0)[:length]
    return conv_out, corr_out


def to_groups(array, groups):
    length, width = array.shape
    return array.reshape(length, groups, width // groups).transpose(1, 0, 2)


def from_groups(array):
    groups, length, width = array.shape
    return array.transpose(1, 0, 2).reshape(length, groups * width)


def reference(query, key_proj, value, filt, skip, cotangent, suffix_start, layer_input, in_weight):
    length = query.shape[0]
    positions = jnp.arange(length, dtype=jnp.int32)
    kept = (positions >= suffix_start[0]).astype(jnp.float32)[:, None]
    grad_out = cotangent.astype(jnp.float32) * kept
    mixed = key_proj.astype(jnp.float32) * value.astype(jnp.float32)
    grad_mixed_in = grad_out * query.astype(jnp.float32)
    groups = 8
    conv_groups, corr_groups = lax.map(convolve_pair, (to_groups(mixed, groups), to_groups(grad_mixed_in, groups), to_groups(filt, groups)))
    conv_out = from_groups(conv_groups)
    corr_out = from_groups(corr_groups)
    mixed_out = conv_out + skip[None, :] * mixed
    grad_query = grad_out * mixed_out
    grad_mixed = corr_out + skip[None, :] * grad_mixed_in
    grad_key = grad_mixed * value.astype(jnp.float32)
    grad_value = grad_mixed * key_proj.astype(jnp.float32)
    grads = jnp.concatenate([grad_query, grad_key, grad_value], axis=1).astype(jnp.bfloat16)
    blocks = 16
    grads_blocks = grads.reshape(blocks, length // blocks, grads.shape[1])
    input_blocks = layer_input.reshape(blocks, length // blocks, layer_input.shape[1])

    def one_block(pair):
        rows_grad, rows_input = pair
        full_grad = jnp.dot(rows_grad, in_weight, preferred_element_type=jnp.float32)
        score = jnp.sum(full_grad * rows_input.astype(jnp.float32), axis=1)
        return full_grad.astype(jnp.bfloat16), score

    input_grad, attribution = lax.map(one_block, (grads_blocks, input_blocks))
    return input_grad.reshape(length, layer_input.shape[1]), attribution.reshape(length)
```

```python
import functools

import jax
import jax.numpy as jnp
import numpy as np
from jax import lax
from jax.experimental import pallas as pl
from jax.experimental.pallas import tpu as pltpu
from jax.sharding import PartitionSpec as P

BF16 = jnp.bfloat16
F32 = jnp.float32
MESH = pl.DeviceIdType.MESH
LANES = 128
GROUP = 8


def split_high_low(table):
    high = table.astype(np.float32).astype(BF16)
    low = (table - high.astype(np.float64)).astype(np.float32).astype(BF16)
    return high, low


def transform_tables(sources, tokens):
    chips = sources // 2
    order = np.arange(sources)
    place = 2 * (order % chips) + order // chips
    odd = np.arange(sources) + 0.5
    angle_one = 2.0 * np.pi / (2 * sources) * (odd[:, None] * place[None, :])
    first = np.concatenate([np.cos(angle_one), -np.sin(angle_one)], axis=0)
    length = 2 * sources * tokens
    turn = 2.0 * np.pi / length * (odd[:, None] * np.arange(tokens)[None, :])
    angle_two = 2.0 * np.pi / tokens * (np.arange(tokens)[:, None] * np.arange(tokens)[None, :] % tokens)
    cos_two, sin_two = np.cos(angle_two), np.sin(angle_two)
    second = np.block([[cos_two, -sin_two], [sin_two, cos_two]])
    back = first.T * (2.0 / length)
    tables = []
    tables += split_high_low(first)
    tables += split_high_low(second)
    tables += split_high_low(second.T)
    tables += split_high_low(back)
    tables += [np.cos(turn).astype(np.float32), np.sin(turn).astype(np.float32)]
    return tables


def halves(array):
    high = array.astype(BF16)
    return high, (array - high.astype(F32)).astype(BF16)


def dot(left, right):
    return jnp.dot(left, right, preferred_element_type=F32)


def to_blocks(signal, chips):
    turned = signal.T
    left = turned[:, :LANES].reshape(chips, GROUP, LANES)
    right = turned[:, LANES:].reshape(chips, GROUP, LANES)
    return jnp.concatenate([left, right], axis=1).astype(BF16)


def from_blocks(blocks, chips):
    blocks = blocks.astype(F32)
    left = blocks[:, :GROUP].reshape(chips * GROUP, LANES)
    right = blocks[:, GROUP:].reshape(chips * GROUP, LANES)
    return jnp.concatenate([left.T, right.T], axis=0)


def conv_kernel(
    chips,
    query, key_proj, value, filt, cotangent, skip, suffix_start,
    one_hi, one_lo, two_hi, two_lo, inv_hi, inv_lo, back_hi, back_lo, turn_cos, turn_sin,
    grads,
    send, recv, rows_f32, flat, spec_hi, spec_lo, spec, time_hi, time_lo, results, outgoing, returned,
    send_sem, recv_sem, pair_sem, send_back_sem, recv_back_sem, pair_back_sem,
):
    sources = 2 * chips
    tokens, width = query.shape
    me = lax.axis_index("seq")
    chip = me // 2
    core = lax.rem(me, 2)
    partner = 2 * chip + (1 - core)

    def peer(step):
        return lax.rem(chip + step, chips)

    barrier = pltpu.get_barrier_semaphore()

    def greet(step, carry):
        pl.semaphore_signal(barrier, inc=1, device_id={"seq": 2 * peer(step) + core}, device_id_type=MESH)
        return carry

    lax.fori_loop(1, chips, greet, 0)
    pl.semaphore_signal(barrier, inc=1, device_id={"seq": partner}, device_id_type=MESH)

    keys = key_proj[...].astype(F32)
    values = value[...].astype(F32)
    mixed = keys * values
    positions = me * tokens + lax.broadcasted_iota(jnp.int32, (tokens, width), 0)
    grad_out = jnp.where(positions >= suffix_start[0], cotangent[...].astype(F32), 0.0)
    grad_mixed_in = grad_out * query[...].astype(F32)
    send[:, 0:16, :] = to_blocks(mixed, chips)
    send[:, 16:32, :] = to_blocks(filt[...], chips)
    send[:, 32:48, :] = to_blocks(grad_mixed_in, chips)

    pl.semaphore_wait(barrier, chips)

    def forward(step, index):
        return pltpu.make_async_remote_copy(
            src_ref=send.at[peer(step)],
            dst_ref=recv.at[core, index],
            send_sem=send_sem.at[step],
            recv_sem=recv_sem.at[index],
            device_id={"seq": 2 * peer(step) + core},
            device_id_type=MESH,
        )

    def start_forward(step, carry):
        forward(step, chip).start()
        return carry

    lax.fori_loop(1, chips, start_forward, 0)
    recv[core, chip] = send[chip]

    def end_forward(step, carry):
        copy = forward(step, peer(step))
        copy.wait_recv()
        copy.wait_send()
        return carry

    lax.fori_loop(1, chips, end_forward, 0)

    theirs = pl.ds(pl.multiple_of(16 * (1 - core), 16), 32)
    swap = pltpu.make_async_remote_copy(
        src_ref=recv.at[core, :, theirs],
        dst_ref=recv.at[core, :, theirs],
        send_sem=pair_sem.at[0],
        recv_sem=pair_sem.at[1],
        device_id={"seq": partner},
        device_id_type=MESH,
    )
    swap.start()
    swap.wait()

    sign = jnp.where(core == 0, 1.0, -1.0).astype(F32)
    for signal in range(2):
        if signal == 0:
            rows = recv[:, :, 16:32, :]
        else:
            rows = recv[:, :, pl.ds(pl.multiple_of(32 * core, 16), 16), :]
        rows_f32[...] = rows.astype(F32).reshape(sources * 16, LANES)
        for r in range(16):
            flat[:, r * LANES : (r + 1) * LANES] = rows_f32[pl.ds(r, sources, stride=16), :].astype(BF16)
        one = dot(one_hi[...], flat[...]) + dot(one_lo[...], flat[...])
        for r in range(16):
            half, channel = r // GROUP, r % GROUP
            columns = slice(half * LANES, (half + 1) * LANES)
            real = one[:sources, r * LANES : (r + 1) * LANES]
            imag = one[sources:, r * LANES : (r + 1) * LANES]
            cos, sin = turn_cos[:, columns], turn_sin[:, columns]
            place = slice((signal * GROUP + channel) * sources, (signal * GROUP + channel + 1) * sources)
            spec_hi[place, columns], spec_lo[place, columns] = halves(real * cos + imag * sin)
            columns = slice(tokens + half * LANES, tokens + (half + 1) * LANES)
            spec_hi[place, columns], spec_lo[place, columns] = halves(imag * cos - real * sin)
    spec[...] = (
        dot(spec_hi[...], two_hi[...]) + dot(spec_lo[...], two_hi[...]) + dot(spec_hi[...], two_lo[...])
    )
    count = GROUP * sources
    fr, fi = spec[:count, :tokens], spec[:count, tokens:] * sign
    pr, pi = spec[count:, :tokens], spec[count:, tokens:]
    product = jnp.concatenate([fr * pr - fi * pi, fr * pi + fi * pr], axis=1)
    prod_hi, prod_lo = halves(product)
    inverse = dot(prod_hi, inv_hi[...]) + dot(prod_lo, inv_hi[...]) + dot(prod_hi, inv_lo[...])
    for r in range(16):
        half, channel = r // GROUP, r % GROUP
        columns = slice(half * LANES, (half + 1) * LANES)
        place = slice(channel * sources, (channel + 1) * sources)
        real = inverse[place, columns]
        imag = inverse[place, tokens + half * LANES : tokens + (half + 1) * LANES]
        cos, sin = turn_cos[:, columns], turn_sin[:, columns]
        columns = slice(r * LANES, (r + 1) * LANES)
        time_hi[:sources, columns], time_lo[:sources, columns] = halves(real * cos - imag * sin)
        time_hi[sources:, columns], time_lo[sources:, columns] = halves(imag * cos + real * sin)
    result = dot(back_hi[...], time_hi[...]) + dot(back_lo[...], time_hi[...]) + dot(back_hi[...], time_lo[...])
    for r in range(16):
        rows_f32[pl.ds(r, sources, stride=16), :] = result[:, r * LANES : (r + 1) * LANES]
    results[...] = rows_f32[...].reshape(2, chips, 16, LANES).astype(BF16)

    mine = pl.ds(pl.multiple_of(16 * core, 16), 16)
    swap_back = pltpu.make_async_remote_copy(
        src_ref=results.at[1 - core],
        dst_ref=outgoing.at[:, mine],
        send_sem=pair_back_sem.at[0],
        recv_sem=pair_back_sem.at[1],
        device_id={"seq": partner},
        device_id_type=MESH,
    )
    swap_back.start()
    outgoing[:, mine, :] = results[core]
    swap_back.wait()

    def backward(step, index):
        return pltpu.make_async_remote_copy(
            src_ref=outgoing.at[peer(step)],
            dst_ref=returned.at[index],
            send_sem=send_back_sem.at[step],
            recv_sem=recv_back_sem.at[index],
            device_id={"seq": 2 * peer(step) + core},
            device_id_type=MESH,
        )

    def start_backward(step, carry):
        backward(step, chip).start()
        return carry

    lax.fori_loop(1, chips, start_backward, 0)
    returned[chip] = outgoing[chip]

    def end_backward(step, carry):
        copy = backward(step, peer(step))
        copy.wait_recv()
        copy.wait_send()
        return carry

    lax.fori_loop(1, chips, end_backward, 0)

    keys = key_proj[...].astype(F32)
    values = value[...].astype(F32)
    gains = skip[...]
    positions = me * tokens + lax.broadcasted_iota(jnp.int32, (tokens, width), 0)
    grad_out = jnp.where(positions >= suffix_start[0], cotangent[...].astype(F32), 0.0)
    conv_out = from_blocks(returned[:, 0:16, :], chips)
    grads[:, :width] = (grad_out * (conv_out + gains * (keys * values))).astype(BF16)
    grad_mixed_in = grad_out * query[...].astype(F32)
    grad_mixed = from_blocks(returned[:, 16:32, :], chips) + gains * grad_mixed_in
    grads[:, width : 2 * width] = (grad_mixed * values).astype(BF16)
    grads[:, 2 * width :] = (grad_mixed * keys).astype(BF16)


def projection_grads(query, key_proj, value, filt, cotangent, skip, suffix_start):
    tokens, width = query.shape
    sources = lax.axis_size("seq")
    chips = sources // 2
    tables = transform_tables(sources, tokens)
    vmem = pl.BlockSpec(memory_space=pltpu.VMEM)
    smem = pl.BlockSpec(memory_space=pltpu.SMEM)
    count = GROUP * sources
    return pl.pallas_call(
        functools.partial(conv_kernel, chips),
        out_shape=jax.ShapeDtypeStruct((tokens, 3 * width), BF16),
        in_specs=[vmem] * 6 + [smem] + [vmem] * len(tables),
        out_specs=vmem,
        scratch_shapes=[
            pltpu.VMEM((chips, 48, LANES), BF16),
            pltpu.VMEM((2, chips, 48, LANES), BF16),
            pltpu.VMEM((sources * 16, LANES), F32),
            pltpu.VMEM((sources, 16 * LANES), BF16),
            pltpu.VMEM((2 * count, 2 * tokens), BF16),
            pltpu.VMEM((2 * count, 2 * tokens), BF16),
            pltpu.VMEM((2 * count, 2 * tokens), F32),
            pltpu.VMEM((2 * sources, 16 * LANES), BF16),
            pltpu.VMEM((2 * sources, 16 * LANES), BF16),
            pltpu.VMEM((2, chips, 16, LANES), BF16),
            pltpu.VMEM((chips, 32, LANES), BF16),
            pltpu.VMEM((chips, 32, LANES), BF16),
            pltpu.SemaphoreType.DMA((chips,)),
            pltpu.SemaphoreType.DMA((chips,)),
            pltpu.SemaphoreType.DMA((2,)),
            pltpu.SemaphoreType.DMA((chips,)),
            pltpu.SemaphoreType.DMA((chips,)),
            pltpu.SemaphoreType.DMA((2,)),
        ],
        compiler_params=pltpu.CompilerParams(
            collective_id=0, has_side_effects=True, vmem_limit_bytes=48 * 1024 * 1024
        ),
        name="conv_grads",
    )(query, key_proj, value, filt, cotangent, skip, suffix_start, *[jnp.asarray(t) for t in tables])


def shards(query, key_proj, value, filt, skip, cotangent, suffix_start, layer_input, in_weight):
    tokens, width = query.shape
    grads = projection_grads(query, key_proj, value, filt, cotangent, skip[None, :], suffix_start)
    features = in_weight.shape[1]
    weights = in_weight.reshape(3, in_weight.shape[0] // 3, features)
    gathered = lax.all_gather(grads, "ch", axis=0)
    gathered = gathered.reshape(-1, tokens, 3, width)
    full_grad = jnp.einsum(
        "atjc,jacd->td",
        gathered,
        weights.reshape(3, -1, width, features),
        preferred_element_type=F32,
    )
    partial_score = jnp.sum(full_grad * layer_input.astype(F32), axis=1)
    attribution = lax.psum(partial_score, "ch")
    return full_grad.astype(BF16), attribution


def solution(mesh):
    in_specs = (
        P("seq", "ch"),
        P("seq", "ch"),
        P("seq", "ch"),
        P("seq", "ch"),
        P("ch"),
        P("seq", "ch"),
        P(),
        P("seq", "ch"),
        P(None, "ch"),
    )
    out_specs = (P("seq", "ch"), P("seq"))
    return jax.shard_map(shards, mesh=mesh, in_specs=in_specs, out_specs=out_specs, check_vma=False)
```

```python
import functools

import jax
import jax.numpy as jnp
import numpy as np
from jax import lax
from jax.experimental import pallas as pl
from jax.experimental.pallas import tpu as pltpu
from jax.sharding import PartitionSpec as P

BF16 = jnp.bfloat16
F32 = jnp.float32
MESH = pl.DeviceIdType.MESH
LANES = 128
GROUP = 8


def split_high_low(table):
    high = table.astype(np.float32).astype(BF16)
    low = (table - high.astype(np.float64)).astype(np.float32).astype(BF16)
    return high, low


def transform_tables(sources, tokens):
    chips = sources // 2
    order = np.arange(sources)
    place = 2 * (order % chips) + order // chips
    odd = np.arange(sources) + 0.5
    angle_one = 2.0 * np.pi / (2 * sources) * (odd[:, None] * place[None, :])
    first = np.concatenate([np.cos(angle_one), -np.sin(angle_one)], axis=0)
    length = 2 * sources * tokens
    turn = 2.0 * np.pi / length * (odd[:, None] * np.arange(tokens)[None, :])
    angle_two = 2.0 * np.pi / tokens * (np.arange(tokens)[:, None] * np.arange(tokens)[None, :] % tokens)
    cos_two, sin_two = np.cos(angle_two), np.sin(angle_two)
    second = np.block([[cos_two, -sin_two], [sin_two, cos_two]])
    back = first.T * (2.0 / length)
    tables = []
    tables += split_high_low(first)
    tables += split_high_low(second)
    tables += split_high_low(second.T)
    tables += split_high_low(back)
    tables += [np.cos(turn).astype(np.float32), np.sin(turn).astype(np.float32)]
    return tables


def halves(array):
    high = array.astype(BF16)
    return high, (array - high.astype(F32)).astype(BF16)


def dot(left, right):
    return jnp.dot(left, right, preferred_element_type=F32)


def to_blocks(signal, chips):
    turned = signal.T
    left = turned[:, :LANES].reshape(chips, GROUP, LANES)
    right = turned[:, LANES:].reshape(chips, GROUP, LANES)
    return jnp.concatenate([left, right], axis=1).astype(BF16)


def from_blocks(blocks, chips):
    blocks = blocks.astype(F32)
    left = blocks[:, :GROUP].reshape(chips * GROUP, LANES)
    right = blocks[:, GROUP:].reshape(chips * GROUP, LANES)
    return jnp.concatenate([left.T, right.T], axis=0)


def conv_kernel(
    chips,
    query, key_proj, value, filt, cotangent, skip, suffix_start,
    one_hi, one_lo, two_hi, two_lo, inv_hi, inv_lo, back_hi, back_lo, turn_cos, turn_sin,
    grads,
    send, recv, rows_f32, flat, spec_hi, spec_lo, spec, time_hi, time_lo, results, outgoing, returned,
    send_sem, recv_sem, pair_sem, send_back_sem, recv_back_sem, pair_back_sem,
):
    sources = 2 * chips
    tokens, width = query.shape
    me = lax.axis_index("seq")
    chip = me // 2
    core = lax.rem(me, 2)
    partner = 2 * chip + (1 - core)

    def peer(step):
        return lax.rem(chip + step, chips)

    barrier = pltpu.get_barrier_semaphore()

    def greet(step, carry):
        pl.semaphore_signal(barrier, inc=1, device_id={"seq": 2 * peer(step) + core}, device_id_type=MESH)
        return carry

    lax.fori_loop(1, chips, greet, 0)
    pl.semaphore_signal(barrier, inc=1, device_id={"seq": partner}, device_id_type=MESH)

    keys = key_proj[...].astype(F32)
    values = value[...].astype(F32)
    mixed = keys * values
    positions = me * tokens + lax.broadcasted_iota(jnp.int32, (tokens, width), 0)
    grad_out = jnp.where(positions >= suffix_start[0], cotangent[...].astype(F32), 0.0)
    grad_mixed_in = grad_out * query[...].astype(F32)
    send[:, 0:16, :] = to_blocks(mixed, chips)
    send[:, 16:32, :] = to_blocks(filt[...], chips)
    send[:, 32:48, :] = to_blocks(grad_mixed_in, chips)

    pl.semaphore_wait(barrier, chips)

    def forward(step, index):
        return pltpu.make_async_remote_copy(
            src_ref=send.at[peer(step)],
            dst_ref=recv.at[core, index],
            send_sem=send_sem.at[step],
            recv_sem=recv_sem.at[index],
            device_id={"seq": 2 * peer(step) + core},
            device_id_type=MESH,
        )

    def start_forward(step, carry):
        forward(step, chip).start()
        return carry

    lax.fori_loop(1, chips, start_forward, 0)
    recv[core, chip] = send[chip]

    def end_forward(step, carry):
        copy = forward(step, peer(step))
        copy.wait_recv()
        copy.wait_send()
        return carry

    lax.fori_loop(1, chips, end_forward, 0)

    theirs = pl.ds(pl.multiple_of(16 * (1 - core), 16), 32)
    swap = pltpu.make_async_remote_copy(
        src_ref=recv.at[core, :, theirs],
        dst_ref=recv.at[core, :, theirs],
        send_sem=pair_sem.at[0],
        recv_sem=pair_sem.at[1],
        device_id={"seq": partner},
        device_id_type=MESH,
    )
    swap.start()
    swap.wait()

    sign = jnp.where(core == 0, 1.0, -1.0).astype(F32)
    for signal in range(2):
        if signal == 0:
            rows = recv[:, :, 16:32, :]
        else:
            rows = recv[:, :, pl.ds(pl.multiple_of(32 * core, 16), 16), :]
        rows_f32[...] = rows.astype(F32).reshape(sources * 16, LANES)
        for r in range(16):
            flat[:, r * LANES : (r + 1) * LANES] = rows_f32[pl.ds(r, sources, stride=16), :].astype(BF16)
        one = dot(one_hi[...], flat[...]) + dot(one_lo[...], flat[...])
        for r in range(16):
            half, channel = r // GROUP, r % GROUP
            columns = slice(half * LANES, (half + 1) * LANES)
            real = one[:sources, r * LANES : (r + 1) * LANES]
            imag = one[sources:, r * LANES : (r + 1) * LANES]
            cos, sin = turn_cos[:, columns], turn_sin[:, columns]
            place = slice((signal * GROUP + channel) * sources, (signal * GROUP + channel + 1) * sources)
            spec_hi[place, columns], spec_lo[place, columns] = halves(real * cos + imag * sin)
            columns = slice(tokens + half * LANES, tokens + (half + 1) * LANES)
            spec_hi[place, columns], spec_lo[place, columns] = halves(imag * cos - real * sin)
    spec[...] = (
        dot(spec_hi[...], two_hi[...]) + dot(spec_lo[...], two_hi[...]) + dot(spec_hi[...], two_lo[...])
    )
    count = GROUP * sources
    fr, fi = spec[:count, :tokens], spec[:count, tokens:] * sign
    pr, pi = spec[count:, :tokens], spec[count:, tokens:]
    product = jnp.concatenate([fr * pr - fi * pi, fr * pi + fi * pr], axis=1)
    prod_hi, prod_lo = halves(product)
    inverse = dot(prod_hi, inv_hi[...]) + dot(prod_lo, inv_hi[...]) + dot(prod_hi, inv_lo[...])
    for r in range(16):
        half, channel = r // GROUP, r % GROUP
        columns = slice(half * LANES, (half + 1) * LANES)
        place = slice(channel * sources, (channel + 1) * sources)
        real = inverse[place, columns]
        imag = inverse[place, tokens + half * LANES : tokens + (half + 1) * LANES]
        cos, sin = turn_cos[:, columns], turn_sin[:, columns]
        columns = slice(r * LANES, (r + 1) * LANES)
        time_hi[:sources, columns], time_lo[:sources, columns] = halves(real * cos - imag * sin)
        time_hi[sources:, columns], time_lo[sources:, columns] = halves(imag * cos + real * sin)
    result = dot(back_hi[...], time_hi[...]) + dot(back_lo[...], time_hi[...]) + dot(back_hi[...], time_lo[...])
    for r in range(16):
        rows_f32[pl.ds(r, sources, stride=16), :] = result[:, r * LANES : (r + 1) * LANES]
    results[...] = rows_f32[...].reshape(2, chips, 16, LANES).astype(BF16)

    mine = pl.ds(pl.multiple_of(16 * core, 16), 16)
    swap_back = pltpu.make_async_remote_copy(
        src_ref=results.at[1 - core],
        dst_ref=outgoing.at[:, mine],
        send_sem=pair_back_sem.at[0],
        recv_sem=pair_back_sem.at[1],
        device_id={"seq": partner},
        device_id_type=MESH,
    )
    swap_back.start()
    outgoing[:, mine, :] = results[core]
    swap_back.wait()

    def backward(step, index):
        return pltpu.make_async_remote_copy(
            src_ref=outgoing.at[peer(step)],
            dst_ref=returned.at[index],
            send_sem=send_back_sem.at[step],
            recv_sem=recv_back_sem.at[index],
            device_id={"seq": 2 * peer(step) + core},
            device_id_type=MESH,
        )

    def start_backward(step, carry):
        backward(step, chip).start()
        return carry

    lax.fori_loop(1, chips, start_backward, 0)
    returned[chip] = outgoing[chip]

    def end_backward(step, carry):
        copy = backward(step, peer(step))
        copy.wait_recv()
        copy.wait_send()
        return carry

    lax.fori_loop(1, chips, end_backward, 0)

    keys = key_proj[...].astype(F32)
    values = value[...].astype(F32)
    gains = skip[...]
    positions = me * tokens + lax.broadcasted_iota(jnp.int32, (tokens, width), 0)
    grad_out = jnp.where(positions >= suffix_start[0], cotangent[...].astype(F32), 0.0)
    conv_out = from_blocks(returned[:, 0:16, :], chips)
    grads[:, :width] = (grad_out * (conv_out + gains * (keys * values))).astype(BF16)
    grad_mixed_in = grad_out * query[...].astype(F32)
    grad_mixed = from_blocks(returned[:, 16:32, :], chips) + gains * grad_mixed_in
    grads[:, width : 2 * width] = (grad_mixed * values).astype(BF16)
    grads[:, 2 * width :] = (grad_mixed * keys).astype(BF16)


def projection_grads(query, key_proj, value, filt, cotangent, skip, suffix_start):
    tokens, width = query.shape
    sources = lax.axis_size("seq")
    chips = sources // 2
    tables = transform_tables(sources, tokens)
    vmem = pl.BlockSpec(memory_space=pltpu.VMEM)
    smem = pl.BlockSpec(memory_space=pltpu.SMEM)
    count = GROUP * sources
    return pl.pallas_call(
        functools.partial(conv_kernel, chips),
        out_shape=jax.ShapeDtypeStruct((tokens, 3 * width), BF16),
        in_specs=[vmem] * 6 + [smem] + [vmem] * len(tables),
        out_specs=vmem,
        scratch_shapes=[
            pltpu.VMEM((chips, 48, LANES), BF16),
            pltpu.VMEM((2, chips, 48, LANES), BF16),
            pltpu.VMEM((sources * 16, LANES), F32),
            pltpu.VMEM((sources, 16 * LANES), BF16),
            pltpu.VMEM((2 * count, 2 * tokens), BF16),
            pltpu.VMEM((2 * count, 2 * tokens), BF16),
            pltpu.VMEM((2 * count, 2 * tokens), F32),
            pltpu.VMEM((2 * sources, 16 * LANES), BF16),
            pltpu.VMEM((2 * sources, 16 * LANES), BF16),
            pltpu.VMEM((2, chips, 16, LANES), BF16),
            pltpu.VMEM((chips, 32, LANES), BF16),
            pltpu.VMEM((chips, 32, LANES), BF16),
            pltpu.SemaphoreType.DMA((chips,)),
            pltpu.SemaphoreType.DMA((chips,)),
            pltpu.SemaphoreType.DMA((2,)),
            pltpu.SemaphoreType.DMA((chips,)),
            pltpu.SemaphoreType.DMA((chips,)),
            pltpu.SemaphoreType.DMA((2,)),
        ],
        compiler_params=pltpu.CompilerParams(
            collective_id=0, has_side_effects=True, vmem_limit_bytes=48 * 1024 * 1024
        ),
        name="conv_grads",
    )(query, key_proj, value, filt, cotangent, skip, suffix_start, *[jnp.asarray(t) for t in tables])


def project_kernel(
    columns,
    grads, own_weight, other_weight, layer_input,
    input_grad, attribution,
    gathered, partial, arrived, scores,
    send_sem, recv_sem, part_sem, score_send_sem, score_recv_sem,
):
    tokens, features = layer_input.shape
    depth = grads.shape[1]
    me = lax.axis_index("ch")
    column, side = me // 2, lax.rem(me, 2)
    partner = 2 * column + (1 - side)
    peers = 2 * columns

    barrier = pltpu.get_barrier_semaphore()
    for step in range(1, peers):
        pl.semaphore_signal(barrier, inc=1, device_id={"ch": lax.rem(me + step, peers)}, device_id_type=MESH)
    pl.semaphore_wait(barrier, peers - 1)

    def gather(step):
        return pltpu.make_async_remote_copy(
            src_ref=grads,
            dst_ref=gathered.at[step],
            send_sem=send_sem.at[step],
            recv_sem=recv_sem.at[step],
            device_id={"ch": 2 * lax.rem(column + columns - step, columns) + side},
            device_id_type=MESH,
        )

    for step in range(1, columns):
        gather(step).start()

    def block(weight, step):
        place = lax.rem(column + step, columns) * depth
        return weight[pl.ds(pl.multiple_of(place, depth), depth), :]

    other = dot(grads[...], block(other_weight, 0))
    own = dot(grads[...], block(own_weight, 0))
    for step in range(1, columns):
        gather(step).wait_recv()
        other += dot(gathered[step], block(other_weight, step))
        if step < columns - 1:
            own += dot(gathered[step], block(own_weight, step))
    partial[...] = other.astype(BF16)
    exchange = pltpu.make_async_remote_copy(
        src_ref=partial,
        dst_ref=arrived,
        send_sem=part_sem.at[0],
        recv_sem=part_sem.at[1],
        device_id={"ch": partner},
        device_id_type=MESH,
    )
    exchange.start()
    if columns > 1:
        own += dot(gathered[columns - 1], block(own_weight, columns - 1))
    exchange.wait()
    full_grad = own + arrived[...].astype(F32)
    input_grad[...] = full_grad.astype(BF16)
    weighted = full_grad * layer_input[...].astype(F32)
    folded = weighted[:, :LANES]
    for start in range(LANES, features, LANES):
        folded = folded + weighted[:, start : start + LANES]
    score = jnp.sum(folded.T, axis=0, keepdims=True)
    scores[me] = jnp.broadcast_to(score, (8, tokens))

    def share(step, index):
        return pltpu.make_async_remote_copy(
            src_ref=scores.at[me],
            dst_ref=scores.at[index],
            send_sem=score_send_sem.at[step],
            recv_sem=score_recv_sem.at[index],
            device_id={"ch": lax.rem(me + step, peers)},
            device_id_type=MESH,
        )

    for step in range(1, peers):
        share(step, me).start()
    for step in range(1, peers):
        copy = share(step, lax.rem(me + step, peers))
        copy.wait_recv()
        copy.wait_send()
    total = scores[0]
    for index in range(1, peers):
        total = total + scores[index]
    attribution[...] = total[0:1, :]
    for step in range(1, columns):
        gather(step).wait_send()


def project(grads, own_weight, other_weight, layer_input):
    tokens, features = layer_input.shape
    peers = lax.axis_size("ch")
    columns = peers // 2
    vmem = pl.BlockSpec(memory_space=pltpu.VMEM)
    return pl.pallas_call(
        functools.partial(project_kernel, columns),
        out_shape=(jax.ShapeDtypeStruct((tokens, features), BF16), jax.ShapeDtypeStruct((1, tokens), F32)),
        in_specs=[vmem] * 4,
        out_specs=(vmem, vmem),
        scratch_shapes=[
            pltpu.VMEM((columns, tokens, grads.shape[1]), BF16),
            pltpu.VMEM((tokens, features), BF16),
            pltpu.VMEM((tokens, features), BF16),
            pltpu.VMEM((peers, 8, tokens), F32),
            pltpu.SemaphoreType.DMA((columns,)),
            pltpu.SemaphoreType.DMA((columns,)),
            pltpu.SemaphoreType.DMA((2,)),
            pltpu.SemaphoreType.DMA((peers,)),
            pltpu.SemaphoreType.DMA((peers,)),
        ],
        compiler_params=pltpu.CompilerParams(
            collective_id=1, has_side_effects=True, vmem_limit_bytes=48 * 1024 * 1024
        ),
        name="project",
    )(grads, own_weight, other_weight, layer_input)


def sided_weights(in_weight, width):
    peers = lax.axis_size("ch")
    parts = lax.axis_size("seq")
    features = in_weight.shape[1]
    side = lax.axis_index("ch") % 2
    rows = in_weight.reshape(3, peers // 2, 2, width, features).transpose(2, 1, 0, 3, 4).reshape(2, -1, features)
    own = lax.dynamic_index_in_dim(rows, side, 0, keepdims=False)
    theirs = lax.dynamic_index_in_dim(rows, 1 - side, 0, keepdims=False)
    share = theirs.shape[0] // parts
    mine = lax.dynamic_slice_in_dim(theirs, lax.axis_index("seq") * share, share, 0)
    swapped = lax.ppermute(mine, "ch", [(i, i ^ 1) for i in range(peers)])
    return own, lax.all_gather(swapped, "seq", axis=0, tiled=True)


def shards(query, key_proj, value, filt, skip, cotangent, suffix_start, layer_input, in_weight):
    tokens, width = query.shape
    own, other = sided_weights(in_weight, width)
    grads = projection_grads(query, key_proj, value, filt, cotangent, skip[None, :], suffix_start)
    input_grad, attribution = project(grads, own, other, layer_input)
    return input_grad, attribution[0]


def solution(mesh):
    in_specs = (
        P("seq", "ch"),
        P("seq", "ch"),
        P("seq", "ch"),
        P("seq", "ch"),
        P("ch"),
        P("seq", "ch"),
        P(),
        P("seq", "ch"),
        P(None, "ch"),
    )
    out_specs = (P("seq", "ch"), P("seq"))
    return jax.shard_map(shards, mesh=mesh, in_specs=in_specs, out_specs=out_specs, check_vma=False)
```

```python
import functools

import jax
import jax.numpy as jnp
import numpy as np
from jax import lax
from jax.experimental import pallas as pl
from jax.experimental.pallas import tpu as pltpu
from jax.sharding import PartitionSpec as P

BF16 = jnp.bfloat16
F32 = jnp.float32
MESH = pl.DeviceIdType.MESH
LANES = 128
GROUP = 8
LINE = 8


def split_high_low(table):
    high = table.astype(np.float32).astype(BF16)
    low = (table - high.astype(np.float64)).astype(np.float32).astype(BF16)
    return high, low


def transform_tables(sources, tokens):
    chips = sources // 2
    order = np.arange(sources)
    place = 2 * (order % chips) + order // chips
    odd = np.arange(sources) + 0.5
    angle_one = 2.0 * np.pi / (2 * sources) * (odd[:, None] * place[None, :])
    first = np.concatenate([np.cos(angle_one), -np.sin(angle_one)], axis=0)
    length = 2 * sources * tokens
    turn = 2.0 * np.pi / length * (odd[:, None] * np.arange(tokens)[None, :])
    angle_two = 2.0 * np.pi / tokens * (np.arange(tokens)[:, None] * np.arange(tokens)[None, :] % tokens)
    cos_two, sin_two = np.cos(angle_two), np.sin(angle_two)
    second = np.block([[cos_two, -sin_two], [sin_two, cos_two]])
    back = first.T * (2.0 / length)
    tables = [np.concatenate(split_high_low(first), axis=1)]
    tables += split_high_low(second)
    tables += split_high_low(second.T)
    tables += split_high_low(back)
    tables += [np.cos(turn).astype(np.float32), np.sin(turn).astype(np.float32)]
    return tables


def halves(array):
    high = array.astype(BF16)
    return high, (array - high.astype(F32)).astype(BF16)


def dot(left, right):
    return jnp.dot(left, right, preferred_element_type=F32)


def to_blocks(signal, chips):
    turned = signal.T
    left = turned[:, :LANES].reshape(chips, GROUP, LANES)
    right = turned[:, LANES:].reshape(chips, GROUP, LANES)
    return jnp.concatenate([left, right], axis=1).astype(BF16)


def far_first(count):
    middle = count // 2
    return sorted(range(count), key=lambda step: (abs(step - middle), step))


def kernel(
    chips, columns,
    query_hbm, key_hbm, value_hbm, filt_hbm, cotangent_hbm, input_hbm, weight_hbm,
    one_hbm, two_hi_hbm, two_lo_hbm, inv_hi_hbm, inv_lo_hbm, back_hi_hbm, back_lo_hbm, cos_hbm, sin_hbm,
    skip, suffix_start,
    input_grad, attribution,
    query, key_proj, value, filt, cotangent, layer_input, own_weight, other_weight,
    one, two_hi, two_lo, inv_hi, inv_lo, back_hi, back_lo, turn_cos, turn_sin,
    send, recv, rows_f32, flat, spec_hi, spec_lo, spec, time_hi, time_lo, results, swapped, outgoing, returned,
    grads, gathered, partial, arrived, totals, scores,
    load_sem, send_sem, recv_sem, pair_sem, send_back_sem, recv_back_sem, pair_back_sem,
    share_sem, line_send_sem, line_recv_sem, ring_send_sem, ring_recv_sem, core_sem,
    gather_send_sem, gather_recv_sem, part_send_sem, part_recv_sem, score_send_sem, score_recv_sem,
):
    sources = 2 * chips
    line = min(LINE, chips)
    rings = chips // line
    peers = 2 * columns
    tokens, width = query.shape
    me, lane = lax.axis_index("seq"), lax.axis_index("ch")
    chip, core = me // 2, lax.rem(me, 2)
    y, z = chip // line, lax.rem(chip, line)
    column, side = lane // 2, lax.rem(lane, 2)

    def seat(dy, dz):
        return lax.rem(y + dy + rings, rings) * line + lax.rem(z + dz + line, line)

    def same_core(dy, dz):
        return {"seq": 2 * seat(dy, dz) + core}

    other_core = {"seq": 2 * chip + (1 - core)}
    other_side = {"ch": 2 * column + (1 - side)}

    def along_x(step):
        return {"ch": 2 * lax.rem(column + step + columns, columns) + side}

    def along_ch(step):
        return {"ch": lax.rem(lane + step + peers, peers)}

    barrier = pltpu.get_barrier_semaphore()

    def over_chips(body):
        for dz in far_first(line):
            def one_step(dy, carry, dz=dz):
                body(dy, dz)
                return carry

            lax.fori_loop(1 if dz == 0 else 0, rings, one_step, 0)

    def greet(device):
        pl.semaphore_signal(barrier, inc=1, device_id=device, device_id_type=MESH)

    over_chips(lambda dy, dz: greet(same_core(dy, dz)))
    greet(other_core)
    for step in range(1, peers):
        greet(along_ch(step))

    loads = [
        (key_hbm, key_proj), (value_hbm, value), (filt_hbm, filt), (cotangent_hbm, cotangent), (query_hbm, query),
        (one_hbm, one), (cos_hbm, turn_cos), (sin_hbm, turn_sin), (two_hi_hbm, two_hi), (two_lo_hbm, two_lo),
        (inv_hi_hbm, inv_hi), (inv_lo_hbm, inv_lo), (back_hi_hbm, back_hi), (back_lo_hbm, back_lo),
        (input_hbm, layer_input),
    ]
    loads += [(weight_hbm.at[:, 2 * index + side], own_weight.at[index]) for index in range(columns)]
    loads = [pltpu.make_async_copy(a, b, load_sem.at[i]) for i, (a, b) in enumerate(loads)]
    for load in loads:
        load.start()

    loads[0].wait()
    loads[1].wait()
    send[:, 0:16, :] = to_blocks(key_proj[...].astype(F32) * value[...].astype(F32), chips)
    loads[2].wait()
    send[:, 16:32, :] = to_blocks(filt[...], chips)
    loads[3].wait()
    loads[4].wait()
    positions = me * tokens + lax.broadcasted_iota(jnp.int32, (tokens, width), 0)
    grad_out = jnp.where(positions >= suffix_start[0], cotangent[...].astype(F32), 0.0)
    send[:, 32:48, :] = to_blocks(grad_out * query[...].astype(F32), chips)

    pl.semaphore_wait(barrier, chips + peers - 1)

    def forward(dy, dz, index):
        return pltpu.make_async_remote_copy(
            src_ref=send.at[seat(dy, dz)],
            dst_ref=recv.at[core, index],
            send_sem=send_sem.at[dy * line + dz],
            recv_sem=recv_sem.at[dy * line + dz],
            device_id=same_core(dy, dz),
            device_id_type=MESH,
        )

    over_chips(lambda dy, dz: forward(dy, dz, chip).start())

    per_column = sources // columns
    share_rows = width // per_column
    share = core * chips + chip
    share_column = share // per_column

    def rows_at(index, count):
        return pl.ds(pl.multiple_of(lax.rem(index, per_column) * share_rows, share_rows), count * share_rows)

    give_share = pltpu.make_async_remote_copy(
        src_ref=weight_hbm.at[:, 2 * share_column + (1 - side), rows_at(share, 1)],
        dst_ref=other_weight.at[share_column, :, rows_at(share, 1)],
        send_sem=share_sem.at[0],
        recv_sem=share_sem.at[1],
        device_id=other_side,
        device_id_type=MESH,
    )
    give_share.start()
    recv[core, chip] = send[chip]
    over_chips(lambda dy, dz: forward(dy, dz, seat(-dy, -dz)).wait_recv())

    theirs = pl.ds(pl.multiple_of(16 * (1 - core), 16), 32)
    swap = pltpu.make_async_remote_copy(
        src_ref=recv.at[core, :, theirs],
        dst_ref=recv.at[core, :, theirs],
        send_sem=pair_sem.at[0],
        recv_sem=pair_sem.at[1],
        device_id=other_core,
        device_id_type=MESH,
    )
    swap.start()

    def along_line(step, index):
        place = other_weight.at[share_column, :, rows_at(core * chips + y * line + index, 1)]
        return pltpu.make_async_remote_copy(
            src_ref=place,
            dst_ref=place,
            send_sem=line_send_sem.at[step],
            recv_sem=line_recv_sem.at[step],
            device_id=same_core(0, step),
            device_id_type=MESH,
        )

    give_share.wait_recv()
    for step in range(1, line):
        along_line(step, z).start()
    swap.wait_recv()

    for index in range(5, 14):
        loads[index].wait()
    sign = jnp.where(core == 0, 1.0, -1.0).astype(F32)
    for signal in range(2):
        if signal == 0:
            rows = recv[:, :, 16:32, :]
        else:
            rows = recv[:, :, pl.ds(pl.multiple_of(32 * core, 16), 16), :]
        rows_f32[...] = rows.astype(F32).reshape(sources * 16, LANES)
        for r in range(16):
            block = rows_f32[pl.ds(r, sources, stride=16), :].astype(BF16)
            flat[:sources, r * LANES : (r + 1) * LANES] = block
            flat[sources:, r * LANES : (r + 1) * LANES] = block
        stage = dot(one[...], flat[...])
        for r in range(16):
            half, channel = r // GROUP, r % GROUP
            span = slice(half * LANES, (half + 1) * LANES)
            real = stage[:sources, r * LANES : (r + 1) * LANES]
            imag = stage[sources:, r * LANES : (r + 1) * LANES]
            cos, sin = turn_cos[:, span], turn_sin[:, span]
            place = slice((signal * GROUP + channel) * sources, (signal * GROUP + channel + 1) * sources)
            spec_hi[place, span], spec_lo[place, span] = halves(real * cos + imag * sin)
            span = slice(tokens + half * LANES, tokens + (half + 1) * LANES)
            spec_hi[place, span], spec_lo[place, span] = halves(imag * cos - real * sin)
    spec[...] = (
        dot(spec_hi[...], two_hi[...]) + dot(spec_lo[...], two_hi[...]) + dot(spec_hi[...], two_lo[...])
    )
    count = GROUP * sources
    fr, fi = spec[:count, :tokens], spec[:count, tokens:] * sign
    pr, pi = spec[count:, :tokens], spec[count:, tokens:]
    product = jnp.concatenate([fr * pr - fi * pi, fr * pi + fi * pr], axis=1)
    prod_hi, prod_lo = halves(product)
    inverse = dot(prod_hi, inv_hi[...]) + dot(prod_lo, inv_hi[...]) + dot(prod_hi, inv_lo[...])
    for r in range(16):
        half, channel = r // GROUP, r % GROUP
        span = slice(half * LANES, (half + 1) * LANES)
        place = slice(channel * sources, (channel + 1) * sources)
        real = inverse[place, span]
        imag = inverse[place, tokens + half * LANES : tokens + (half + 1) * LANES]
        cos, sin = turn_cos[:, span], turn_sin[:, span]
        span = slice(r * LANES, (r + 1) * LANES)
        time_hi[:sources, span], time_lo[:sources, span] = halves(real * cos - imag * sin)
        time_hi[sources:, span], time_lo[sources:, span] = halves(imag * cos + real * sin)
    result = dot(back_hi[...], time_hi[...]) + dot(back_lo[...], time_hi[...]) + dot(back_hi[...], time_lo[...])
    for r in range(16):
        rows_f32[pl.ds(r, sources, stride=16), :] = result[:, r * LANES : (r + 1) * LANES]
    results[...] = rows_f32[...].reshape(2, chips, 16, LANES).astype(BF16)

    swap_back = pltpu.make_async_remote_copy(
        src_ref=results.at[1 - core],
        dst_ref=swapped,
        send_sem=pair_back_sem.at[0],
        recv_sem=pair_back_sem.at[1],
        device_id=other_core,
        device_id_type=MESH,
    )
    swap_back.start()

    def along_ring(step, index):
        first = core * chips + index * line
        place = other_weight.at[first // per_column, :, rows_at(first, line)]
        return pltpu.make_async_remote_copy(
            src_ref=place,
            dst_ref=place,
            send_sem=ring_send_sem.at[step],
            recv_sem=ring_recv_sem.at[step],
            device_id=same_core(step, 0),
            device_id_type=MESH,
        )

    mine = results[core].astype(F32)
    swap_back.wait_recv()
    given = swapped[...].astype(F32)
    conv = jnp.where(core == 0, mine, given)
    corr = jnp.where(core == 0, given, mine)
    for half in range(2):
        span = slice(half * GROUP, (half + 1) * GROUP)
        outgoing[half] = jnp.concatenate([conv[:, span], corr[:, span]], axis=1).astype(BF16)

    def backward(half, dy, dz, index):
        return pltpu.make_async_remote_copy(
            src_ref=outgoing.at[half, seat(dy, dz)],
            dst_ref=returned.at[half, index],
            send_sem=send_back_sem.at[half, dy * line + dz],
            recv_sem=recv_back_sem.at[half, dy * line + dz],
            device_id=same_core(dy, dz),
            device_id_type=MESH,
        )

    for half in range(2):
        over_chips(lambda dy, dz: backward(half, dy, dz, chip).start())
        returned[half, chip] = outgoing[half, chip]
    for step in range(1, line):
        along_line(step, lax.rem(z - step + line, line)).wait_recv()
    for step in range(1, rings):
        along_ring(step, y).start()

    def gather(half, step):
        return pltpu.make_async_remote_copy(
            src_ref=grads.at[half],
            dst_ref=gathered.at[half, step],
            send_sem=gather_send_sem.at[half, step],
            recv_sem=gather_recv_sem.at[half, step],
            device_id=along_x(-step),
            device_id_type=MESH,
        )

    gains = skip[...]
    for half in range(2):
        over_chips(lambda dy, dz: backward(half, dy, dz, seat(-dy, -dz)).wait_recv())
        span = slice(half * LANES, (half + 1) * LANES)
        blocks = returned[half].astype(F32)
        conv_out = blocks[:, :GROUP].reshape(width, LANES).T
        corr_out = blocks[:, GROUP:].reshape(width, LANES).T
        keys = key_proj[span, :].astype(F32)
        values = value[span, :].astype(F32)
        positions = me * tokens + half * LANES + lax.broadcasted_iota(jnp.int32, (LANES, width), 0)
        grad_out = jnp.where(positions >= suffix_start[0], cotangent[span, :].astype(F32), 0.0)
        grad_mixed = corr_out + gains * (grad_out * query[span, :].astype(F32))
        grads[half, :, :width] = (grad_out * (conv_out + gains * (keys * values))).astype(BF16)
        grads[half, :, width : 2 * width] = (grad_mixed * values).astype(BF16)
        grads[half, :, 2 * width :] = (grad_mixed * keys).astype(BF16)
        for step in range(1, columns):
            gather(half, step).start()

    for step in range(1, rings):
        along_ring(step, lax.rem(y - step + rings, rings)).wait_recv()
    portion = other_weight.at[pl.ds(core * (columns // 2), columns // 2)]
    give_core = pltpu.make_async_remote_copy(
        src_ref=portion,
        dst_ref=portion,
        send_sem=core_sem.at[0],
        recv_sem=core_sem.at[1],
        device_id=other_core,
        device_id_type=MESH,
    )
    give_core.start()
    for index in range(14, len(loads)):
        loads[index].wait()
    give_core.wait_recv()

    def exchange(half):
        return pltpu.make_async_remote_copy(
            src_ref=partial.at[half],
            dst_ref=arrived.at[half],
            send_sem=part_send_sem.at[half],
            recv_sem=part_recv_sem.at[half],
            device_id=other_side,
            device_id_type=MESH,
        )

    def product_of(half, step, weight):
        left = grads[half] if step == 0 else gathered[half, step]
        return dot(left, weight[lax.rem(column + step, columns)].reshape(3 * width, -1))

    for half in range(2):
        other = product_of(half, 0, other_weight)
        own = product_of(half, 0, own_weight)
        for step in range(1, columns):
            gather(half, step).wait_recv()
            other += product_of(half, step, other_weight)
        partial[half] = other.astype(BF16)
        exchange(half).start()
        for step in range(1, columns):
            own += product_of(half, step, own_weight)
        totals[half] = own

    parts = []
    for half in range(2):
        span = slice(half * LANES, (half + 1) * LANES)
        exchange(half).wait_recv()
        full_grad = totals[half] + arrived[half].astype(F32)
        input_grad[span, :] = full_grad.astype(BF16)
        weighted = full_grad * layer_input[span, :].astype(F32)
        features = weighted.shape[1]
        folded = weighted[:, : min(LANES, features)]
        for start in range(LANES, features, LANES):
            folded = folded + weighted[:, start : start + LANES]
        parts.append(jnp.sum(folded.T, axis=0, keepdims=True))
    scores[lane] = jnp.broadcast_to(jnp.concatenate(parts, axis=1), (8, tokens))

    def tell(step, index):
        return pltpu.make_async_remote_copy(
            src_ref=scores.at[index],
            dst_ref=scores.at[index],
            send_sem=score_send_sem.at[step],
            recv_sem=score_recv_sem.at[step],
            device_id=along_ch(step),
            device_id_type=MESH,
        )

    for step in range(1, peers):
        tell(step, lane).start()

    over_chips(lambda dy, dz: forward(dy, dz, chip).wait_send())
    give_share.wait_send()
    swap.wait_send()
    swap_back.wait_send()
    give_core.wait_send()
    for step in range(1, line):
        along_line(step, z).wait_send()
    for step in range(1, rings):
        along_ring(step, y).wait_send()
    for half in range(2):
        over_chips(lambda dy, dz: backward(half, dy, dz, chip).wait_send())
        for step in range(1, columns):
            gather(half, step).wait_send()
        exchange(half).wait_send()

    for step in range(1, peers):
        tell(step, lax.rem(lane - step + peers, peers)).wait_recv()
    total = scores[0]
    for index in range(1, peers):
        total = total + scores[index]
    attribution[...] = total[0:1, :]
    for step in range(1, peers):
        tell(step, lane).wait_send()


def shards(query, key_proj, value, filt, skip, cotangent, suffix_start, layer_input, in_weight):
    tokens, width = query.shape
    features = in_weight.shape[1]
    sources, peers = lax.axis_size("seq"), lax.axis_size("ch")
    chips, columns = sources // 2, peers // 2
    line = min(LINE, chips)
    rings = chips // line
    tables = transform_tables(sources, tokens)
    count = GROUP * sources
    vmem = pl.BlockSpec(memory_space=pltpu.VMEM)
    smem = pl.BlockSpec(memory_space=pltpu.SMEM)
    hbm = pl.BlockSpec(memory_space=pl.ANY)
    dma = pltpu.SemaphoreType.DMA
    block = pltpu.VMEM((tokens, width), BF16)
    weight_block = pltpu.VMEM((columns, 3, width, features), BF16)
    input_grad, attribution = pl.pallas_call(
        functools.partial(kernel, chips, columns),
        out_shape=(jax.ShapeDtypeStruct((tokens, features), BF16), jax.ShapeDtypeStruct((1, tokens), F32)),
        in_specs=[hbm] * (7 + len(tables)) + [vmem, smem],
        out_specs=(vmem, vmem),
        scratch_shapes=[
            block, block, block, pltpu.VMEM((tokens, width), F32), block, pltpu.VMEM((tokens, features), BF16),
            weight_block, weight_block,
            *[pltpu.VMEM(table.shape, table.dtype) for table in tables],
            pltpu.VMEM((chips, 48, LANES), BF16),
            pltpu.VMEM((2, chips, 48, LANES), BF16),
            pltpu.VMEM((sources * 16, LANES), F32),
            pltpu.VMEM((2 * sources, 16 * LANES), BF16),
            pltpu.VMEM((2 * count, 2 * tokens), BF16),
            pltpu.VMEM((2 * count, 2 * tokens), BF16),
            pltpu.VMEM((2 * count, 2 * tokens), F32),
            pltpu.VMEM((2 * sources, 16 * LANES), BF16),
            pltpu.VMEM((2 * sources, 16 * LANES), BF16),
            pltpu.VMEM((2, chips, 16, LANES), BF16),
            pltpu.VMEM((chips, 16, LANES), BF16),
            pltpu.VMEM((2, chips, 16, LANES), BF16),
            pltpu.VMEM((2, chips, 16, LANES), BF16),
            pltpu.VMEM((2, LANES, 3 * width), BF16),
            pltpu.VMEM((2, columns, LANES, 3 * width), BF16),
            pltpu.VMEM((2, LANES, features), BF16),
            pltpu.VMEM((2, LANES, features), BF16),
            pltpu.VMEM((2, LANES, features), F32),
            pltpu.VMEM((peers, 8, tokens), F32),
            dma((15 + columns,)),
            dma((chips,)), dma((chips,)), dma((2,)),
            dma((2, chips)), dma((2, chips)), dma((2,)),
            dma((2,)), dma((line,)), dma((line,)), dma((rings,)), dma((rings,)), dma((2,)),
            dma((2, columns)), dma((2, columns)), dma((2,)), dma((2,)), dma((peers,)), dma((peers,)),
        ],
        compiler_params=pltpu.CompilerParams(
            collective_id=0, has_side_effects=True, vmem_limit_bytes=56 * 1024 * 1024
        ),
        name="conv_backward",
    )(
        query, key_proj, value, filt, cotangent, layer_input, in_weight.reshape(3, peers, width, features),
        *[jnp.asarray(table) for table in tables],
        skip[None, :], suffix_start,
    )
    return input_grad, attribution[0]


def solution(mesh):
    in_specs = (
        P("seq", "ch"),
        P("seq", "ch"),
        P("seq", "ch"),
        P("seq", "ch"),
        P("ch"),
        P("seq", "ch"),
        P(),
        P("seq", "ch"),
        P(None, "ch"),
    )
    out_specs = (P("seq", "ch"), P("seq"))
    return jax.shard_map(shards, mesh=mesh, in_specs=in_specs, out_specs=out_specs, check_vma=False)
```

```python
import functools

import jax
import jax.numpy as jnp
import numpy as np
from jax import lax
from jax.experimental import pallas as pl
from jax.experimental.pallas import tpu as pltpu
from jax.sharding import PartitionSpec as P

BF16 = jnp.bfloat16
F32 = jnp.float32
MESH = pl.DeviceIdType.MESH
LANES = 128
GROUP = 8
LINE = 8
PART = 64


def split_high_low(table):
    high = table.astype(np.float32).astype(BF16)
    low = (table - high.astype(np.float64)).astype(np.float32).astype(BF16)
    return high, low


def transform_tables(sources, tokens):
    chips = sources // 2
    order = np.arange(sources)
    place = 2 * (order % chips) + order // chips
    odd = np.arange(sources) + 0.5
    angle_one = 2.0 * np.pi / (2 * sources) * (odd[:, None] * place[None, :])
    first = np.concatenate([np.cos(angle_one), -np.sin(angle_one)], axis=0)
    length = 2 * sources * tokens
    turn = 2.0 * np.pi / length * (odd[:, None] * np.arange(tokens)[None, :])
    angle_two = 2.0 * np.pi / tokens * (np.arange(tokens)[:, None] * np.arange(tokens)[None, :] % tokens)
    cos_two, sin_two = np.cos(angle_two), np.sin(angle_two)
    second = np.block([[cos_two, -sin_two], [sin_two, cos_two]])
    back = first.T * (2.0 / length)
    tables = [np.concatenate(split_high_low(first), axis=1)]
    tables += split_high_low(second)
    tables += split_high_low(second.T)
    tables += split_high_low(back)
    tables += [np.cos(turn).astype(np.float32), np.sin(turn).astype(np.float32)]
    return tables


def halves(array):
    high = array.astype(BF16)
    return high, (array - high.astype(F32)).astype(BF16)


def dot(left, right):
    return jnp.dot(left, right, preferred_element_type=F32)


def to_blocks(signal, chips):
    turned = signal.T
    left = turned[:, :LANES].reshape(chips, GROUP, LANES)
    right = turned[:, LANES:].reshape(chips, GROUP, LANES)
    return jnp.concatenate([left, right], axis=1).astype(BF16)


def far_first(count):
    middle = count // 2
    return sorted(range(count), key=lambda step: (abs(step - middle), step))


def kernel(
    chips, columns,
    query_hbm, key_hbm, value_hbm, filt_hbm, cotangent_hbm, input_hbm, weight_hbm,
    one_hbm, two_hi_hbm, two_lo_hbm, inv_hi_hbm, inv_lo_hbm, back_hi_hbm, back_lo_hbm, cos_hbm, sin_hbm,
    skip, suffix_start,
    input_grad, attribution,
    query, key_proj, value, filt, cotangent, layer_input, other_input, own_weight, other_weight,
    one, two_hi, two_lo, inv_hi, inv_lo, back_hi, back_lo, turn_cos, turn_sin,
    send, recv, rows_f32, flat, spec_hi, spec_lo, spec, time_hi, time_lo, results, swapped, outgoing, returned,
    grads, gathered, partial, arrived, totals, others, scores,
    load_sem, send_sem, recv_sem, pair_sem, send_back_sem, recv_back_sem, pair_back_sem,
    share_sem, line_send_sem, line_recv_sem, ring_send_sem, ring_recv_sem, core_sem,
    input_sem,
    gather_send_sem, gather_recv_sem, hand_send_sem, hand_recv_sem, part_send_sem, part_recv_sem, score_send_sem, score_recv_sem,
):
    sources = 2 * chips
    line = min(LINE, chips)
    rings = chips // line
    peers = 2 * columns
    tokens, width = query.shape
    me, lane = lax.axis_index("seq"), lax.axis_index("ch")
    chip, core = me // 2, lax.rem(me, 2)
    y, z = chip // line, lax.rem(chip, line)
    column, side = lane // 2, lax.rem(lane, 2)

    def seat(dy, dz):
        return lax.rem(y + dy + rings, rings) * line + lax.rem(z + dz + line, line)

    def same_core(dy, dz):
        return {"seq": 2 * seat(dy, dz) + core}

    other_core = {"seq": 2 * chip + (1 - core)}
    other_side = {"ch": 2 * column + (1 - side)}

    def along_x(step):
        return {"ch": 2 * lax.rem(column + step + columns, columns) + side}

    def along_ch(step):
        return {"ch": lax.rem(lane + step + peers, peers)}

    barrier = pltpu.get_barrier_semaphore()

    def over_chips(body):
        for dz in far_first(line):
            def one_step(dy, carry, dz=dz):
                body(dy, dz)
                return carry

            lax.fori_loop(1 if dz == 0 else 0, rings, one_step, 0)

    def greet(device):
        pl.semaphore_signal(barrier, inc=1, device_id=device, device_id_type=MESH)

    for step in range(1, peers):
        greet(along_ch(step))
    over_chips(lambda dy, dz: greet(same_core(dy, dz)))
    greet(other_core)
    loads = [
        (key_hbm, key_proj), (value_hbm, value), (filt_hbm, filt), (cotangent_hbm, cotangent), (query_hbm, query),
        (one_hbm, one), (cos_hbm, turn_cos), (sin_hbm, turn_sin), (two_hi_hbm, two_hi), (two_lo_hbm, two_lo),
        (inv_hi_hbm, inv_hi), (inv_lo_hbm, inv_lo), (back_hi_hbm, back_hi), (back_lo_hbm, back_lo),
        (input_hbm, layer_input),
    ]
    loads += [(weight_hbm.at[:, 2 * index + side], own_weight.at[index]) for index in range(columns)]
    loads = [pltpu.make_async_copy(a, b, load_sem.at[i]) for i, (a, b) in enumerate(loads)]
    for load in loads:
        load.start()

    loads[0].wait()
    loads[1].wait()
    send[:, 0:16, :] = to_blocks(key_proj[...].astype(F32) * value[...].astype(F32), chips)
    loads[2].wait()
    send[:, 16:32, :] = to_blocks(filt[...], chips)
    loads[3].wait()
    loads[4].wait()
    positions = me * tokens + lax.broadcasted_iota(jnp.int32, (tokens, width), 0)
    grad_out = jnp.where(positions >= suffix_start[0], cotangent[...].astype(F32), 0.0)
    send[:, 32:48, :] = to_blocks(grad_out * query[...].astype(F32), chips)

    pl.semaphore_wait(barrier, chips + peers - 1)

    def forward(dy, dz, index):
        return pltpu.make_async_remote_copy(
            src_ref=send.at[seat(dy, dz)],
            dst_ref=recv.at[core, index],
            send_sem=send_sem.at[dy * line + dz],
            recv_sem=recv_sem.at[dy * line + dz],
            device_id=same_core(dy, dz),
            device_id_type=MESH,
        )

    per_column = sources // columns
    share_rows = width // per_column
    share = core * chips + chip
    share_column = share // per_column

    def rows_at(index, count):
        return pl.ds(pl.multiple_of(lax.rem(index, per_column) * share_rows, share_rows), count * share_rows)

    give_share = pltpu.make_async_remote_copy(
        src_ref=weight_hbm.at[:, 2 * share_column + (1 - side), rows_at(share, 1)],
        dst_ref=other_weight.at[share_column, :, rows_at(share, 1)],
        send_sem=share_sem.at[0],
        recv_sem=share_sem.at[1],
        device_id=other_side,
        device_id_type=MESH,
    )
    give_share.start()
    over_chips(lambda dy, dz: forward(dy, dz, chip).start())
    recv[core, chip] = send[chip]

    def mirror(index, distance):
        return index + distance * (1 - 2 * lax.rem(index // distance, 2))

    def along_line(step, block, owner):
        place = other_weight.at[share_column, :, rows_at(core * chips + y * line + (mirror(owner) if block else owner), 1)]
        target = mirror(z) if step == 0 else ahead(step)
        return pltpu.make_async_remote_copy(
            src_ref=place,
            dst_ref=place,
            send_sem=line_send_sem.at[2 * step + block],
            recv_sem=line_recv_sem.at[2 * step + block],
            device_id=same_core(0, target - z),
            device_id_type=MESH,
        )

    half_line = line // 2
    within = [(step, block) for step in range(1, half_line) for block in range(2)]

    def mirror(index):
        return index + half_line * (1 - 2 * (index // half_line))

    def ahead(step):
        return z // half_line * half_line + lax.rem(z + step + half_line, half_line)

    give_share.wait_recv()
    if half_line:
        along_line(0, 0, z).start()
    over_chips(lambda dy, dz: forward(dy, dz, seat(-dy, -dz)).wait_recv())

    theirs = pl.ds(pl.multiple_of(16 * (1 - core), 16), 32)
    swap = pltpu.make_async_remote_copy(
        src_ref=recv.at[core, :, theirs],
        dst_ref=recv.at[core, :, theirs],
        send_sem=pair_sem.at[0],
        recv_sem=pair_sem.at[1],
        device_id=other_core,
        device_id_type=MESH,
    )
    swap.start()

    swap.wait_recv()
    if half_line:
        along_line(0, 0, mirror(z)).wait_recv()
    for step, block in within:
        along_line(step, block, z).start()

    def lend_input():
        place = pl.ds(LANES, LANES)
        return pltpu.make_async_remote_copy(
            src_ref=input_hbm.at[place],
            dst_ref=other_input,
            send_sem=input_sem.at[0],
            recv_sem=input_sem.at[1],
            device_id=other_side,
            device_id_type=MESH,
        )

    for index in range(5, 14):
        loads[index].wait()
    sign = jnp.where(core == 0, 1.0, -1.0).astype(F32)
    for signal in range(2):
        if signal == 0:
            rows = recv[:, :, 16:32, :]
        else:
            rows = recv[:, :, pl.ds(pl.multiple_of(32 * core, 16), 16), :]
        rows_f32[...] = rows.astype(F32).reshape(sources * 16, LANES)
        for r in range(16):
            block = rows_f32[pl.ds(r, sources, stride=16), :].astype(BF16)
            flat[:sources, r * LANES : (r + 1) * LANES] = block
            flat[sources:, r * LANES : (r + 1) * LANES] = block
        stage = dot(one[...], flat[...])
        for r in range(16):
            half, channel = r // GROUP, r % GROUP
            span = slice(half * LANES, (half + 1) * LANES)
            real = stage[:sources, r * LANES : (r + 1) * LANES]
            imag = stage[sources:, r * LANES : (r + 1) * LANES]
            cos, sin = turn_cos[:, span], turn_sin[:, span]
            place = slice((signal * GROUP + channel) * sources, (signal * GROUP + channel + 1) * sources)
            spec_hi[place, span], spec_lo[place, span] = halves(real * cos + imag * sin)
            span = slice(tokens + half * LANES, tokens + (half + 1) * LANES)
            spec_hi[place, span], spec_lo[place, span] = halves(imag * cos - real * sin)
    spec[...] = (
        dot(spec_hi[...], two_hi[...]) + dot(spec_lo[...], two_hi[...]) + dot(spec_hi[...], two_lo[...])
    )
    count = GROUP * sources
    fr, fi = spec[:count, :tokens], spec[:count, tokens:] * sign
    pr, pi = spec[count:, :tokens], spec[count:, tokens:]
    product = jnp.concatenate([fr * pr - fi * pi, fr * pi + fi * pr], axis=1)
    prod_hi, prod_lo = halves(product)
    inverse = dot(prod_hi, inv_hi[...]) + dot(prod_lo, inv_hi[...]) + dot(prod_hi, inv_lo[...])
    for r in range(16):
        half, channel = r // GROUP, r % GROUP
        span = slice(half * LANES, (half + 1) * LANES)
        place = slice(channel * sources, (channel + 1) * sources)
        real = inverse[place, span]
        imag = inverse[place, tokens + half * LANES : tokens + (half + 1) * LANES]
        cos, sin = turn_cos[:, span], turn_sin[:, span]
        span = slice(r * LANES, (r + 1) * LANES)
        time_hi[:sources, span], time_lo[:sources, span] = halves(real * cos - imag * sin)
        time_hi[sources:, span], time_lo[sources:, span] = halves(imag * cos + real * sin)
    result = dot(back_hi[...], time_hi[...]) + dot(back_lo[...], time_hi[...]) + dot(back_hi[...], time_lo[...])
    for r in range(16):
        rows_f32[pl.ds(r, sources, stride=16), :] = result[:, r * LANES : (r + 1) * LANES]
    results[...] = rows_f32[...].reshape(2, chips, 16, LANES).astype(BF16)

    swap_back = pltpu.make_async_remote_copy(
        src_ref=results.at[1 - core],
        dst_ref=swapped,
        send_sem=pair_back_sem.at[0],
        recv_sem=pair_back_sem.at[1],
        device_id=other_core,
        device_id_type=MESH,
    )
    swap_back.start()

    def along_ring(step, index):
        first = core * chips + index * line
        place = other_weight.at[first // per_column, :, rows_at(first, line)]
        return pltpu.make_async_remote_copy(
            src_ref=place,
            dst_ref=place,
            send_sem=ring_send_sem.at[step],
            recv_sem=ring_recv_sem.at[step],
            device_id=same_core(step, 0),
            device_id_type=MESH,
        )

    for step, block in within:
        along_line(step, block, ahead(-step)).wait_recv()
    for step in range(1, rings):
        along_ring(step, y).start()
    mine = results[core].astype(F32)
    swap_back.wait_recv()
    given = swapped[...].astype(F32)
    conv = jnp.where(core == 0, mine, given)
    corr = jnp.where(core == 0, given, mine)
    for half in range(2):
        span = slice(half * GROUP, (half + 1) * GROUP)
        outgoing[half] = jnp.concatenate([conv[:, span], corr[:, span]], axis=1).astype(BF16)

    def backward(half, dy, dz, index):
        return pltpu.make_async_remote_copy(
            src_ref=outgoing.at[half, seat(dy, dz)],
            dst_ref=returned.at[half, index],
            send_sem=send_back_sem.at[half, dy * line + dz],
            recv_sem=recv_back_sem.at[half, dy * line + dz],
            device_id=same_core(dy, dz),
            device_id_type=MESH,
        )

    for half in range(2):
        over_chips(lambda dy, dz: backward(half, dy, dz, chip).start())
        returned[half, chip] = outgoing[half, chip]

    def gather(part, step):
        return pltpu.make_async_remote_copy(
            src_ref=grads.at[part],
            dst_ref=gathered.at[part, step],
            send_sem=gather_send_sem.at[part, step],
            recv_sem=gather_recv_sem.at[part, step],
            device_id=along_x(-step),
            device_id_type=MESH,
        )

    relayed = columns == 4
    near = (1, 3) if relayed else tuple(range(1, columns))

    def hand_on(part, source):
        span = pl.ds(PART // 2, PART // 2) if source == 1 else pl.ds(0, PART // 2)
        return pltpu.make_async_remote_copy(
            src_ref=gathered.at[part, source, span],
            dst_ref=gathered.at[part, 2, span],
            send_sem=hand_send_sem.at[part, source // 2],
            recv_sem=hand_recv_sem.at[part, source // 2],
            device_id=along_x(-source),
            device_id_type=MESH,
        )

    def end_near(half):
        for part in parts_of(half):
            for step in near:
                gather(part, step).wait_recv()
                if relayed:
                    hand_on(part, step).start()

    def parts_of(half):
        return range(half * LANES // PART, (half + 1) * LANES // PART)

    gains = skip[...]
    for half in range(2):
        over_chips(lambda dy, dz: backward(half, dy, dz, seat(-dy, -dz)).wait_recv())
        if half:
            end_near(0)
        span = slice(half * LANES, (half + 1) * LANES)
        blocks = returned[half].astype(F32)
        conv_out = blocks[:, :GROUP].reshape(width, LANES).T
        corr_out = blocks[:, GROUP:].reshape(width, LANES).T
        keys = key_proj[span, :].astype(F32)
        values = value[span, :].astype(F32)
        positions = me * tokens + half * LANES + lax.broadcasted_iota(jnp.int32, (LANES, width), 0)
        grad_out = jnp.where(positions >= suffix_start[0], cotangent[span, :].astype(F32), 0.0)
        grad_mixed = corr_out + gains * (grad_out * query[span, :].astype(F32))
        pieces = (grad_out * (conv_out + gains * (keys * values)), grad_mixed * values, grad_mixed * keys)
        pieces = jnp.concatenate(pieces, axis=1).astype(BF16)
        for index, part in enumerate(parts_of(half)):
            grads[part] = pieces[index * PART : (index + 1) * PART]
            for step in near:
                gather(part, step).start()
    lend_input().start()

    for step in range(1, rings):
        along_ring(step, lax.rem(y - step + rings, rings)).wait_recv()
    portion = other_weight.at[pl.ds(core * (columns // 2), columns // 2)]
    give_core = pltpu.make_async_remote_copy(
        src_ref=portion,
        dst_ref=portion,
        send_sem=core_sem.at[0],
        recv_sem=core_sem.at[1],
        device_id=other_core,
        device_id_type=MESH,
    )
    give_core.start()

    def exchange(part):
        return pltpu.make_async_remote_copy(
            src_ref=partial.at[part],
            dst_ref=arrived.at[part],
            send_sem=part_send_sem.at[part],
            recv_sem=part_recv_sem.at[part],
            device_id=other_side,
            device_id_type=MESH,
        )

    def weight_at(step, weight):
        return weight[lax.rem(column + step, columns)].reshape(3 * width, -1)

    for half in range(2):
        if half:
            end_near(half)
        else:
            give_core.wait_recv()
        rows = slice(parts_of(half)[0], parts_of(half)[-1] + 1)
        other = dot(grads[rows].reshape(LANES, -1), weight_at(0, other_weight))
        for step in near:
            if half == 0 and not relayed:
                for part in parts_of(half):
                    gather(part, step).wait_recv()
            other += dot(gathered[rows, step].reshape(LANES, -1), weight_at(step, other_weight))
        others[half] = other
        for index, part in enumerate(parts_of(half)):
            span = slice(index * PART, (index + 1) * PART)
            if relayed:
                hand_on(part, 1).wait_recv()
                hand_on(part, 3).wait_recv()
                others[half, span] += dot(gathered[part, 2], weight_at(2, other_weight))
            partial[part] = others[half, span].astype(BF16)
            exchange(part).start()

    for index in range(14, len(loads)):
        loads[index].wait()
    for half in range(2):
        rows = slice(parts_of(half)[0], parts_of(half)[-1] + 1)
        own = dot(grads[rows].reshape(LANES, -1), weight_at(0, own_weight))
        for step in range(1, columns):
            own += dot(gathered[rows, step].reshape(LANES, -1), weight_at(step, own_weight))
        totals[half] = own

    def tell(half, step, index):
        return pltpu.make_async_remote_copy(
            src_ref=scores.at[index, half],
            dst_ref=scores.at[index, half],
            send_sem=score_send_sem.at[half, step],
            recv_sem=score_recv_sem.at[half, step],
            device_id=along_ch(step),
            device_id_type=MESH,
        )

    def share_scores(half, weighted):
        features = weighted.shape[1]
        folded = weighted[:, : min(LANES, features)]
        for start in range(LANES, features, LANES):
            folded = folded + weighted[:, start : start + LANES]
        scores[lane, half] = jnp.broadcast_to(jnp.sum(folded.T, axis=0, keepdims=True), (8, LANES))
        for step in range(1, peers):
            tell(half, step, lane).start()

    def finish(half):
        for part in parts_of(half):
            exchange(part).wait_recv()
        rows = slice(parts_of(half)[0], parts_of(half)[-1] + 1)
        full_grad = totals[half] + arrived[rows].astype(F32).reshape(LANES, -1)
        input_grad[half * LANES : (half + 1) * LANES, :] = full_grad.astype(BF16)
        return full_grad

    share_scores(0, finish(0) * layer_input[:LANES, :].astype(F32))
    lend_input().wait_recv()
    share_scores(
        1, totals[1] * layer_input[LANES:, :].astype(F32) + others[1] * other_input[...].astype(F32)
    )
    finish(1)

    over_chips(lambda dy, dz: forward(dy, dz, chip).wait_send())
    give_share.wait_send()
    swap.wait_send()
    swap_back.wait_send()
    give_core.wait_send()
    if half_line:
        along_line(0, 0, z).wait_send()
    for step, block in within:
        along_line(step, block, z).wait_send()
    for step in range(1, rings):
        along_ring(step, y).wait_send()
    for half in range(2):
        over_chips(lambda dy, dz: backward(half, dy, dz, chip).wait_send())
        for part in parts_of(half):
            for step in near:
                gather(part, step).wait_send()
                if relayed:
                    hand_on(part, step).wait_send()
            exchange(part).wait_send()
    lend_input().wait_send()

    for half in range(2):
        for step in range(1, peers):
            tell(half, step, lax.rem(lane - step + peers, peers)).wait_recv()
        total = scores[0, half]
        for index in range(1, peers):
            total = total + scores[index, half]
        attribution[:, half * LANES : (half + 1) * LANES] = total[0:1, :]
    for half in range(2):
        for step in range(1, peers):
            tell(half, step, lane).wait_send()


def shards(query, key_proj, value, filt, skip, cotangent, suffix_start, layer_input, in_weight):
    tokens, width = query.shape
    features = in_weight.shape[1]
    sources, peers = lax.axis_size("seq"), lax.axis_size("ch")
    chips, columns = sources // 2, peers // 2
    line = min(LINE, chips)
    rings = chips // line
    tables = transform_tables(sources, tokens)
    count = GROUP * sources
    parts = tokens // PART
    vmem = pl.BlockSpec(memory_space=pltpu.VMEM)
    smem = pl.BlockSpec(memory_space=pltpu.SMEM)
    hbm = pl.BlockSpec(memory_space=pl.ANY)
    dma = pltpu.SemaphoreType.DMA
    block = pltpu.VMEM((tokens, width), BF16)
    weight_block = pltpu.VMEM((columns, 3, width, features), BF16)
    input_grad, attribution = pl.pallas_call(
        functools.partial(kernel, chips, columns),
        out_shape=(jax.ShapeDtypeStruct((tokens, features), BF16), jax.ShapeDtypeStruct((1, tokens), F32)),
        in_specs=[hbm] * (7 + len(tables)) + [vmem, smem],
        out_specs=(vmem, vmem),
        scratch_shapes=[
            block, block, block, pltpu.VMEM((tokens, width), F32), block,
            pltpu.VMEM((tokens, features), BF16), pltpu.VMEM((LANES, features), BF16),
            weight_block, weight_block,
            *[pltpu.VMEM(table.shape, table.dtype) for table in tables],
            pltpu.VMEM((chips, 48, LANES), BF16),
            pltpu.VMEM((2, chips, 48, LANES), BF16),
            pltpu.VMEM((sources * 16, LANES), F32),
            pltpu.VMEM((2 * sources, 16 * LANES), BF16),
            pltpu.VMEM((2 * count, 2 * tokens), BF16),
            pltpu.VMEM((2 * count, 2 * tokens), BF16),
            pltpu.VMEM((2 * count, 2 * tokens), F32),
            pltpu.VMEM((2 * sources, 16 * LANES), BF16),
            pltpu.VMEM((2 * sources, 16 * LANES), BF16),
            pltpu.VMEM((2, chips, 16, LANES), BF16),
            pltpu.VMEM((chips, 16, LANES), BF16),
            pltpu.VMEM((2, chips, 16, LANES), BF16),
            pltpu.VMEM((2, chips, 16, LANES), BF16),
            pltpu.VMEM((parts, PART, 3 * width), BF16),
            pltpu.VMEM((parts, columns, PART, 3 * width), BF16),
            pltpu.VMEM((parts, PART, features), BF16),
            pltpu.VMEM((parts, PART, features), BF16),
            pltpu.VMEM((2, LANES, features), F32),
            pltpu.VMEM((2, LANES, features), F32),
            pltpu.VMEM((peers, 2, 8, LANES), F32),
            dma((15 + columns,)),
            dma((chips,)), dma((chips,)), dma((2,)),
            dma((2, chips)), dma((2, chips)), dma((2,)),
            dma((2,)), dma((line,)), dma((line,)), dma((rings,)), dma((rings,)), dma((2,)),
            dma((2,)),
            dma((parts, columns)), dma((parts, columns)), dma((parts, 2)), dma((parts, 2)),
            dma((parts,)), dma((parts,)), dma((2, peers)), dma((2, peers)),
        ],
        compiler_params=pltpu.CompilerParams(
            collective_id=0, has_side_effects=True, vmem_limit_bytes=56 * 1024 * 1024
        ),
        name="conv_backward",
    )(
        query, key_proj, value, filt, cotangent, layer_input, in_weight.reshape(3, peers, width, features),
        *[jnp.asarray(table) for table in tables],
        skip[None, :], suffix_start,
    )
    return input_grad, attribution[0]


def solution(mesh):
    in_specs = (
        P("seq", "ch"),
        P("seq", "ch"),
        P("seq", "ch"),
        P("seq", "ch"),
        P("ch"),
        P("seq", "ch"),
        P(),
        P("seq", "ch"),
        P(None, "ch"),
    )
    out_specs = (P("seq", "ch"), P("seq"))
    return jax.shard_map(shards, mesh=mesh, in_specs=in_specs, out_specs=out_specs, check_vma=False)
```

```python
import functools

import jax
import jax.numpy as jnp
import numpy as np
from jax import lax
from jax.experimental import pallas as pl
from jax.experimental.pallas import tpu as pltpu
from jax.sharding import PartitionSpec as P

BF16 = jnp.bfloat16
F32 = jnp.float32
MESH = pl.DeviceIdType.MESH
LANES = 128
GROUP = 8
LINE = 8
PART = 64
EARLIEST = 4096


def split_high_low(table):
    high = table.astype(np.float32).astype(BF16)
    low = (table - high.astype(np.float64)).astype(np.float32).astype(BF16)
    return high, low


def transform_tables(sources, tokens):
    chips = sources // 2
    order = np.arange(sources)
    place = 2 * (order % chips) + order // chips
    odd = np.arange(sources) + 0.5
    angle_one = 2.0 * np.pi / (2 * sources) * (odd[:, None] * place[None, :])
    first = np.concatenate([np.cos(angle_one), -np.sin(angle_one)], axis=0)
    length = 2 * sources * tokens
    turn = 2.0 * np.pi / length * (odd[:, None] * np.arange(tokens)[None, :])
    angle_two = 2.0 * np.pi / tokens * (np.arange(tokens)[:, None] * np.arange(tokens)[None, :] % tokens)
    cos_two, sin_two = np.cos(angle_two), np.sin(angle_two)
    second = np.block([[cos_two, -sin_two], [sin_two, cos_two]])
    back = first.T * (2.0 / length)
    tables = [np.concatenate(split_high_low(first), axis=1)]
    tables += split_high_low(second)
    tables += split_high_low(second.T)
    tables += split_high_low(back)
    tables += [np.cos(turn).astype(np.float32), np.sin(turn).astype(np.float32)]
    return tables


def halves(array):
    high = array.astype(BF16)
    return high, (array - high.astype(F32)).astype(BF16)


def dot(left, right):
    return jnp.dot(left, right, preferred_element_type=F32)


def to_blocks(signal, chips):
    turned = signal.T
    left = turned[:, :LANES].reshape(chips, GROUP, LANES)
    right = turned[:, LANES:].reshape(chips, GROUP, LANES)
    return jnp.concatenate([left, right], axis=1).astype(BF16)


def far_first(count):
    middle = count // 2
    return sorted(range(count), key=lambda step: (abs(step - middle), step))


def kernel(
    chips, columns,
    query_hbm, key_hbm, value_hbm, filt_hbm, cotangent_hbm, input_hbm, weight_hbm,
    one_hbm, two_hi_hbm, two_lo_hbm, inv_hi_hbm, inv_lo_hbm, back_hi_hbm, back_lo_hbm, cos_hbm, sin_hbm,
    skip, suffix_start,
    input_grad, attribution,
    query, key_proj, value, filt, cotangent, layer_input, other_input, own_weight, other_weight,
    one, two_hi, two_lo, inv_hi, inv_lo, back_hi, back_lo, turn_cos, turn_sin,
    send, recv, rows_f32, flat, spec_hi, spec_lo, spec, time_hi, time_lo, results, swapped, outgoing, returned,
    grads, gathered, partial, arrived, totals, others, scores,
    load_sem, send_sem, recv_sem, pair_sem, send_back_sem, recv_back_sem, pair_back_sem,
    share_sem, line_send_sem, line_recv_sem, ring_send_sem, ring_recv_sem, core_sem,
    input_sem,
    gather_send_sem, gather_recv_sem, hand_send_sem, hand_recv_sem, part_send_sem, part_recv_sem, score_send_sem, score_recv_sem,
):
    sources = 2 * chips
    line = min(LINE, chips)
    rings = chips // line
    peers = 2 * columns
    tokens, width = query.shape
    me, lane = lax.axis_index("seq"), lax.axis_index("ch")
    chip, core = me // 2, lax.rem(me, 2)
    y, z = chip // line, lax.rem(chip, line)
    column, side = lane // 2, lax.rem(lane, 2)

    def seat(dy, dz):
        return lax.rem(y + dy + rings, rings) * line + lax.rem(z + dz + line, line)

    def same_core(dy, dz):
        return {"seq": 2 * seat(dy, dz) + core}

    other_core = {"seq": 2 * chip + (1 - core)}
    other_side = {"ch": 2 * column + (1 - side)}

    def along_x(step):
        return {"ch": 2 * lax.rem(column + step + columns, columns) + side}

    def along_ch(step):
        return {"ch": lax.rem(lane + step + peers, peers)}

    barrier = pltpu.get_barrier_semaphore()

    def over_chips(body):
        for dz in far_first(line):
            def one_step(dy, carry, dz=dz):
                body(dy, dz)
                return carry

            lax.fori_loop(1 if dz == 0 else 0, rings, one_step, 0)

    def greet(device):
        pl.semaphore_signal(barrier, inc=1, device_id=device, device_id_type=MESH)

    loads = [
        (key_hbm, key_proj), (value_hbm, value), (filt_hbm, filt), (cotangent_hbm, cotangent), (query_hbm, query),
        (one_hbm, one), (cos_hbm, turn_cos), (sin_hbm, turn_sin), (two_hi_hbm, two_hi), (two_lo_hbm, two_lo),
        (inv_hi_hbm, inv_hi), (inv_lo_hbm, inv_lo), (back_hi_hbm, back_hi), (back_lo_hbm, back_lo),
        (input_hbm, layer_input),
    ]
    loads += [(weight_hbm.at[:, 2 * index + side], own_weight.at[index]) for index in range(columns)]
    loads = [pltpu.make_async_copy(a, b, load_sem.at[i]) for i, (a, b) in enumerate(loads)]
    for load in loads[:5]:
        load.start()
    for step in range(1, peers):
        greet(along_ch(step))
    over_chips(lambda dy, dz: greet(same_core(dy, dz)))
    greet(other_core)
    for load in loads[5:]:
        load.start()

    loads[0].wait()
    loads[1].wait()
    send[:, 0:16, :] = to_blocks(key_proj[...].astype(F32) * value[...].astype(F32), chips)
    loads[2].wait()
    send[:, 16:32, :] = to_blocks(filt[...], chips)
    loads[3].wait()
    loads[4].wait()
    positions = me * tokens + lax.broadcasted_iota(jnp.int32, (tokens, width), 0)
    grad_out = jnp.where(positions >= suffix_start[0], cotangent[...].astype(F32), 0.0)
    send[:, 32:48, :] = to_blocks(grad_out * query[...].astype(F32), chips)

    pl.semaphore_wait(barrier, chips + peers - 1)

    quiet = EARLIEST // (2 * tokens)
    is_quiet = chip < quiet
    rest = chips - quiet

    def forward(dy, dz, short):
        rows = pl.ds(0, 32 if short else 48)
        return pltpu.make_async_remote_copy(
            src_ref=send.at[seat(dy, dz), rows],
            dst_ref=recv.at[core, chip, rows],
            send_sem=send_sem.at[0],
            recv_sem=recv_sem.at[int(short)],
            device_id=same_core(dy, dz),
            device_id_type=MESH,
        )

    def send_signals():
        if quiet:
            @pl.when(is_quiet)
            def _():
                over_chips(lambda dy, dz: forward(dy, dz, True).start())

        @pl.when(jnp.logical_not(is_quiet))
        def _():
            over_chips(lambda dy, dz: forward(dy, dz, False).start())

    def drain(place, semaphore):
        pltpu.make_async_copy(place, place, semaphore).wait()

    def receive_signals(full, short):
        if full:
            drain(recv.at[core, pl.ds(0, full)], recv_sem.at[0])
        if short:
            drain(recv.at[core, pl.ds(0, short), pl.ds(0, 32)], recv_sem.at[1])

    def end_signals():
        if quiet:
            @pl.when(is_quiet)
            def _():
                receive_signals(rest, quiet - 1)

        @pl.when(jnp.logical_not(is_quiet))
        def _():
            receive_signals(rest - 1, quiet)

    def end_sends():
        if quiet and chips > 1:
            @pl.when(is_quiet)
            def _():
                drain(send.at[pl.ds(0, chips - 1), pl.ds(0, 32)], send_sem.at[0])

        @pl.when(jnp.logical_not(is_quiet))
        def _():
            if chips > 1:
                drain(send.at[pl.ds(0, chips - 1)], send_sem.at[0])

    per_column = sources // columns
    share_rows = width // per_column
    share = core * chips + chip
    share_column = share // per_column

    def rows_at(index, count):
        return pl.ds(pl.multiple_of(lax.rem(index, per_column) * share_rows, share_rows), count * share_rows)

    give_share = pltpu.make_async_remote_copy(
        src_ref=weight_hbm.at[:, 2 * share_column + (1 - side), rows_at(share, 1)],
        dst_ref=other_weight.at[share_column, :, rows_at(share, 1)],
        send_sem=share_sem.at[0],
        recv_sem=share_sem.at[1],
        device_id=other_side,
        device_id_type=MESH,
    )
    give_share.start()
    send_signals()
    if quiet:
        recv[core, 0:quiet, 32:48, :] = jnp.zeros((quiet, 16, LANES), BF16)
    recv[core, chip] = send[chip]

    def mirror(index, distance):
        return index + distance * (1 - 2 * lax.rem(index // distance, 2))

    def along_line(step, block, owner):
        place = other_weight.at[share_column, :, rows_at(core * chips + y * line + (mirror(owner) if block else owner), 1)]
        target = mirror(z) if step == 0 else ahead(step)
        return pltpu.make_async_remote_copy(
            src_ref=place,
            dst_ref=place,
            send_sem=line_send_sem.at[2 * step + block],
            recv_sem=line_recv_sem.at[2 * step + block],
            device_id=same_core(0, target - z),
            device_id_type=MESH,
        )

    half_line = line // 2
    within = [(step, block) for step in range(1, half_line) for block in range(2)]

    def mirror(index):
        return index + half_line * (1 - 2 * (index // half_line))

    def ahead(step):
        return z // half_line * half_line + lax.rem(z + step + half_line, half_line)

    give_share.wait_recv()
    if half_line:
        along_line(0, 0, z).start()
    end_signals()

    theirs = pl.ds(pl.multiple_of(16 * (1 - core), 16), 32)
    swap = pltpu.make_async_remote_copy(
        src_ref=recv.at[core, :, theirs],
        dst_ref=recv.at[core, :, theirs],
        send_sem=pair_sem.at[0],
        recv_sem=pair_sem.at[1],
        device_id=other_core,
        device_id_type=MESH,
    )
    swap.start()

    swap.wait_recv()

    def lend_input():
        place = pl.ds(LANES, LANES)
        return pltpu.make_async_remote_copy(
            src_ref=input_hbm.at[place],
            dst_ref=other_input,
            send_sem=input_sem.at[0],
            recv_sem=input_sem.at[1],
            device_id=other_side,
            device_id_type=MESH,
        )

    for index in range(5, 14):
        loads[index].wait()
    sign = jnp.where(core == 0, 1.0, -1.0).astype(F32)
    for signal in range(2):
        if signal == 0:
            rows = recv[:, :, 16:32, :]
        else:
            rows = recv[:, :, pl.ds(pl.multiple_of(32 * core, 16), 16), :]
        rows_f32[...] = rows.astype(F32).reshape(sources * 16, LANES)
        for r in range(16):
            block = rows_f32[pl.ds(r, sources, stride=16), :].astype(BF16)
            flat[:sources, r * LANES : (r + 1) * LANES] = block
            flat[sources:, r * LANES : (r + 1) * LANES] = block
        stage = dot(one[...], flat[...])
        for r in range(16):
            half, channel = r // GROUP, r % GROUP
            span = slice(half * LANES, (half + 1) * LANES)
            real = stage[:sources, r * LANES : (r + 1) * LANES]
            imag = stage[sources:, r * LANES : (r + 1) * LANES]
            cos, sin = turn_cos[:, span], turn_sin[:, span]
            place = slice((signal * GROUP + channel) * sources, (signal * GROUP + channel + 1) * sources)
            spec_hi[place, span], spec_lo[place, span] = halves(real * cos + imag * sin)
            span = slice(tokens + half * LANES, tokens + (half + 1) * LANES)
            spec_hi[place, span], spec_lo[place, span] = halves(imag * cos - real * sin)
    if half_line:
        along_line(0, 0, mirror(z)).wait_recv()
    for step, block in within:
        along_line(step, block, z).start()
    spec[...] = (
        dot(spec_hi[...], two_hi[...]) + dot(spec_lo[...], two_hi[...]) + dot(spec_hi[...], two_lo[...])
    )
    count = GROUP * sources
    fr, fi = spec[:count, :tokens], spec[:count, tokens:] * sign
    pr, pi = spec[count:, :tokens], spec[count:, tokens:]
    product = jnp.concatenate([fr * pr - fi * pi, fr * pi + fi * pr], axis=1)
    prod_hi, prod_lo = halves(product)
    inverse = dot(prod_hi, inv_hi[...]) + dot(prod_lo, inv_hi[...]) + dot(prod_hi, inv_lo[...])
    for r in range(16):
        half, channel = r // GROUP, r % GROUP
        span = slice(half * LANES, (half + 1) * LANES)
        place = slice(channel * sources, (channel + 1) * sources)
        real = inverse[place, span]
        imag = inverse[place, tokens + half * LANES : tokens + (half + 1) * LANES]
        cos, sin = turn_cos[:, span], turn_sin[:, span]
        span = slice(r * LANES, (r + 1) * LANES)
        time_hi[:sources, span], time_lo[:sources, span] = halves(real * cos - imag * sin)
        time_hi[sources:, span], time_lo[sources:, span] = halves(imag * cos + real * sin)
    result = dot(back_hi[...], time_hi[...]) + dot(back_lo[...], time_hi[...]) + dot(back_hi[...], time_lo[...])
    for r in range(16):
        rows_f32[pl.ds(r, sources, stride=16), :] = result[:, r * LANES : (r + 1) * LANES]
    results[...] = rows_f32[...].reshape(2, chips, 16, LANES).astype(BF16)

    swap_back = pltpu.make_async_remote_copy(
        src_ref=results.at[1 - core],
        dst_ref=swapped,
        send_sem=pair_back_sem.at[0],
        recv_sem=pair_back_sem.at[1],
        device_id=other_core,
        device_id_type=MESH,
    )
    swap_back.start()

    def along_ring(step, index):
        first = core * chips + index * line
        place = other_weight.at[first // per_column, :, rows_at(first, line)]
        return pltpu.make_async_remote_copy(
            src_ref=place,
            dst_ref=place,
            send_sem=ring_send_sem.at[step],
            recv_sem=ring_recv_sem.at[step],
            device_id=same_core(step, 0),
            device_id_type=MESH,
        )

    mine = results[core].astype(F32)
    swap_back.wait_recv()
    given = swapped[...].astype(F32)
    conv = jnp.where(core == 0, mine, given)
    corr = jnp.where(core == 0, given, mine)
    for half in range(2):
        span = slice(half * GROUP, (half + 1) * GROUP)
        outgoing[half] = jnp.concatenate([conv[:, span], corr[:, span]], axis=1).astype(BF16)

    def backward(half, dy, dz):
        return pltpu.make_async_remote_copy(
            src_ref=outgoing.at[half, seat(dy, dz)],
            dst_ref=returned.at[half, chip],
            send_sem=send_back_sem.at[half],
            recv_sem=recv_back_sem.at[half],
            device_id=same_core(dy, dz),
            device_id_type=MESH,
        )

    for half in range(2):
        over_chips(lambda dy, dz: backward(half, dy, dz).start())
        returned[half, chip] = outgoing[half, chip]

    for step, block in within:
        along_line(step, block, ahead(-step)).wait_recv()
    for step in range(1, rings):
        along_ring(step, y).start()
    end_sends()
    give_share.wait_send()
    swap.wait_send()
    swap_back.wait_send()
    if half_line:
        along_line(0, 0, z).wait_send()
    for step, block in within:
        along_line(step, block, z).wait_send()

    def gather(part, step):
        return pltpu.make_async_remote_copy(
            src_ref=grads.at[part],
            dst_ref=gathered.at[part, step],
            send_sem=gather_send_sem.at[part, step],
            recv_sem=gather_recv_sem.at[part, step],
            device_id=along_x(-step),
            device_id_type=MESH,
        )

    relayed = columns == 4
    near = (1, 3) if relayed else tuple(range(1, columns))

    def hand_on(part, source):
        span = pl.ds(PART // 2, PART // 2) if source == 1 else pl.ds(0, PART // 2)
        return pltpu.make_async_remote_copy(
            src_ref=gathered.at[part, source, span],
            dst_ref=gathered.at[part, 2, span],
            send_sem=hand_send_sem.at[part, source // 2],
            recv_sem=hand_recv_sem.at[part, source // 2],
            device_id=along_x(-source),
            device_id_type=MESH,
        )

    def end_near(half):
        for part in parts_of(half):
            for step in near:
                gather(part, step).wait_recv()
                if relayed:
                    hand_on(part, step).start()

    def parts_of(half):
        return range(half * LANES // PART, (half + 1) * LANES // PART)

    gains = skip[...]
    for half in range(2):
        if chips > 1:
            drain(returned.at[half, pl.ds(0, chips - 1)], recv_back_sem.at[half])
        if half:
            end_near(0)
        span = slice(half * LANES, (half + 1) * LANES)
        blocks = returned[half].astype(F32)
        conv_out = blocks[:, :GROUP].reshape(width, LANES).T
        corr_out = blocks[:, GROUP:].reshape(width, LANES).T
        keys = key_proj[span, :].astype(F32)
        values = value[span, :].astype(F32)
        positions = me * tokens + half * LANES + lax.broadcasted_iota(jnp.int32, (LANES, width), 0)
        grad_out = jnp.where(positions >= suffix_start[0], cotangent[span, :].astype(F32), 0.0)
        grad_mixed = corr_out + gains * (grad_out * query[span, :].astype(F32))
        pieces = (grad_out * (conv_out + gains * (keys * values)), grad_mixed * values, grad_mixed * keys)
        pieces = jnp.concatenate(pieces, axis=1).astype(BF16)
        for index, part in enumerate(parts_of(half)):
            grads[part] = pieces[index * PART : (index + 1) * PART]
            for step in near:
                gather(part, step).start()
    lend_input().start()

    for step in range(1, rings):
        along_ring(step, lax.rem(y - step + rings, rings)).wait_recv()
    portion = other_weight.at[pl.ds(core * (columns // 2), columns // 2)]
    give_core = pltpu.make_async_remote_copy(
        src_ref=portion,
        dst_ref=portion,
        send_sem=core_sem.at[0],
        recv_sem=core_sem.at[1],
        device_id=other_core,
        device_id_type=MESH,
    )
    give_core.start()

    def exchange(part):
        return pltpu.make_async_remote_copy(
            src_ref=partial.at[part],
            dst_ref=arrived.at[part],
            send_sem=part_send_sem.at[part],
            recv_sem=part_recv_sem.at[part],
            device_id=other_side,
            device_id_type=MESH,
        )

    def weight_at(step, weight):
        return weight[lax.rem(column + step, columns)].reshape(3 * width, -1)

    for half in range(2):
        if half:
            end_near(half)
        else:
            give_core.wait_recv()
        rows = slice(parts_of(half)[0], parts_of(half)[-1] + 1)
        other = dot(grads[rows].reshape(LANES, -1), weight_at(0, other_weight))
        for step in near:
            if half == 0 and not relayed:
                for part in parts_of(half):
                    gather(part, step).wait_recv()
            other += dot(gathered[rows, step].reshape(LANES, -1), weight_at(step, other_weight))
        others[half] = other
        for index, part in enumerate(parts_of(half)):
            span = slice(index * PART, (index + 1) * PART)
            if relayed:
                hand_on(part, 1).wait_recv()
                hand_on(part, 3).wait_recv()
                others[half, span] += dot(gathered[part, 2], weight_at(2, other_weight))
            partial[part] = others[half, span].astype(BF16)
            exchange(part).start()

    for index in range(14, len(loads)):
        loads[index].wait()
    for half in range(2):
        rows = slice(parts_of(half)[0], parts_of(half)[-1] + 1)
        own = dot(grads[rows].reshape(LANES, -1), weight_at(0, own_weight))
        for step in range(1, columns):
            own += dot(gathered[rows, step].reshape(LANES, -1), weight_at(step, own_weight))
        totals[half] = own

    def tell(half, step, index):
        return pltpu.make_async_remote_copy(
            src_ref=scores.at[index, half],
            dst_ref=scores.at[index, half],
            send_sem=score_send_sem.at[half, step],
            recv_sem=score_recv_sem.at[half, step],
            device_id=along_ch(step),
            device_id_type=MESH,
        )

    def share_scores(half, weighted):
        features = weighted.shape[1]
        folded = weighted[:, : min(LANES, features)]
        for start in range(LANES, features, LANES):
            folded = folded + weighted[:, start : start + LANES]
        scores[lane, half] = jnp.broadcast_to(jnp.sum(folded.T, axis=0, keepdims=True), (8, LANES))
        for step in range(1, peers):
            tell(half, step, lane).start()

    def finish(half):
        for part in parts_of(half):
            exchange(part).wait_recv()
        rows = slice(parts_of(half)[0], parts_of(half)[-1] + 1)
        full_grad = totals[half] + arrived[rows].astype(F32).reshape(LANES, -1)
        input_grad[half * LANES : (half + 1) * LANES, :] = full_grad.astype(BF16)
        return full_grad

    give_core.wait_send()
    for step in range(1, rings):
        along_ring(step, y).wait_send()
    for half in range(2):
        if chips > 1:
            drain(outgoing.at[half, pl.ds(0, chips - 1)], send_back_sem.at[half])
        for part in parts_of(half):
            for step in near:
                gather(part, step).wait_send()
                if relayed:
                    hand_on(part, step).wait_send()

    share_scores(0, finish(0) * layer_input[:LANES, :].astype(F32))
    lend_input().wait_recv()
    share_scores(
        1, totals[1] * layer_input[LANES:, :].astype(F32) + others[1] * other_input[...].astype(F32)
    )
    finish(1)
    lend_input().wait_send()
    for part in range(tokens // PART):
        exchange(part).wait_send()

    for half in range(2):
        for step in range(1, peers):
            tell(half, step, lax.rem(lane - step + peers, peers)).wait_recv()
        total = scores[0, half]
        for index in range(1, peers):
            total = total + scores[index, half]
        attribution[:, half * LANES : (half + 1) * LANES] = total[0:1, :]
    for half in range(2):
        for step in range(1, peers):
            tell(half, step, lane).wait_send()


def shards(query, key_proj, value, filt, skip, cotangent, suffix_start, layer_input, in_weight):
    tokens, width = query.shape
    features = in_weight.shape[1]
    sources, peers = lax.axis_size("seq"), lax.axis_size("ch")
    chips, columns = sources // 2, peers // 2
    line = min(LINE, chips)
    rings = chips // line
    tables = transform_tables(sources, tokens)
    count = GROUP * sources
    parts = tokens // PART
    vmem = pl.BlockSpec(memory_space=pltpu.VMEM)
    smem = pl.BlockSpec(memory_space=pltpu.SMEM)
    hbm = pl.BlockSpec(memory_space=pl.ANY)
    dma = pltpu.SemaphoreType.DMA
    block = pltpu.VMEM((tokens, width), BF16)
    weight_block = pltpu.VMEM((columns, 3, width, features), BF16)
    input_grad, attribution = pl.pallas_call(
        functools.partial(kernel, chips, columns),
        out_shape=(jax.ShapeDtypeStruct((tokens, features), BF16), jax.ShapeDtypeStruct((1, tokens), F32)),
        in_specs=[hbm] * (7 + len(tables)) + [vmem, smem],
        out_specs=(vmem, vmem),
        scratch_shapes=[
            block, block, block, pltpu.VMEM((tokens, width), F32), block,
            pltpu.VMEM((tokens, features), BF16), pltpu.VMEM((LANES, features), BF16),
            weight_block, weight_block,
            *[pltpu.VMEM(table.shape, table.dtype) for table in tables],
            pltpu.VMEM((chips, 48, LANES), BF16),
            pltpu.VMEM((2, chips, 48, LANES), BF16),
            pltpu.VMEM((sources * 16, LANES), F32),
            pltpu.VMEM((2 * sources, 16 * LANES), BF16),
            pltpu.VMEM((2 * count, 2 * tokens), BF16),
            pltpu.VMEM((2 * count, 2 * tokens), BF16),
            pltpu.VMEM((2 * count, 2 * tokens), F32),
            pltpu.VMEM((2 * sources, 16 * LANES), BF16),
            pltpu.VMEM((2 * sources, 16 * LANES), BF16),
            pltpu.VMEM((2, chips, 16, LANES), BF16),
            pltpu.VMEM((chips, 16, LANES), BF16),
            pltpu.VMEM((2, chips, 16, LANES), BF16),
            pltpu.VMEM((2, chips, 16, LANES), BF16),
            pltpu.VMEM((parts, PART, 3 * width), BF16),
            pltpu.VMEM((parts, columns, PART, 3 * width), BF16),
            pltpu.VMEM((parts, PART, features), BF16),
            pltpu.VMEM((parts, PART, features), BF16),
            pltpu.VMEM((2, LANES, features), F32),
            pltpu.VMEM((2, LANES, features), F32),
            pltpu.VMEM((peers, 2, 8, LANES), F32),
            dma((15 + columns,)),
            dma((1,)), dma((2,)), dma((2,)),
            dma((2,)), dma((2,)), dma((2,)),
            dma((2,)), dma((line,)), dma((line,)), dma((rings,)), dma((rings,)), dma((2,)),
            dma((2,)),
            dma((parts, columns)), dma((parts, columns)), dma((parts, 2)), dma((parts, 2)),
            dma((parts,)), dma((parts,)), dma((2, peers)), dma((2, peers)),
        ],
        compiler_params=pltpu.CompilerParams(
            collective_id=0, has_side_effects=True, vmem_limit_bytes=56 * 1024 * 1024
        ),
        name="conv_backward",
    )(
        query, key_proj, value, filt, cotangent, layer_input, in_weight.reshape(3, peers, width, features),
        *[jnp.asarray(table) for table in tables],
        skip[None, :], suffix_start,
    )
    return input_grad, attribution[0]


def solution(mesh):
    in_specs = (
        P("seq", "ch"),
        P("seq", "ch"),
        P("seq", "ch"),
        P("seq", "ch"),
        P("ch"),
        P("seq", "ch"),
        P(),
        P("seq", "ch"),
        P(None, "ch"),
    )
    out_specs = (P("seq", "ch"), P("seq"))
    return jax.shard_map(shards, mesh=mesh, in_specs=in_specs, out_specs=out_specs, check_vma=False)
```

```python
import functools

import jax
import jax.numpy as jnp
import numpy as np
from jax import lax
from jax.experimental import pallas as pl
from jax.experimental.pallas import tpu as pltpu
from jax.sharding import PartitionSpec as P

BF16 = jnp.bfloat16
F32 = jnp.float32
MESH = pl.DeviceIdType.MESH
LANES = 128
GROUP = 8
LINE = 8
PART = 64
EARLIEST = 4096


def split_high_low(table):
    high = table.astype(np.float32).astype(BF16)
    low = (table - high.astype(np.float64)).astype(np.float32).astype(BF16)
    return high, low


def transform_tables(sources, tokens):
    chips = sources // 2
    order = np.arange(sources)
    place = 2 * (order % chips) + order // chips
    odd = np.arange(sources) + 0.5
    angle_one = 2.0 * np.pi / (2 * sources) * (odd[:, None] * place[None, :])
    first = np.concatenate([np.cos(angle_one), -np.sin(angle_one)], axis=0)
    length = 2 * sources * tokens
    turn = 2.0 * np.pi / length * (odd[:, None] * np.arange(tokens)[None, :])
    angle_two = 2.0 * np.pi / tokens * (np.arange(tokens)[:, None] * np.arange(tokens)[None, :] % tokens)
    cos_two, sin_two = np.cos(angle_two), np.sin(angle_two)
    second = np.block([[cos_two, -sin_two], [sin_two, cos_two]])
    back = first.T * (2.0 / length)
    tables = [np.concatenate(split_high_low(first), axis=1)]
    tables += split_high_low(second)
    tables += split_high_low(second.T)
    tables += split_high_low(back)
    tables += [np.cos(turn).astype(np.float32), np.sin(turn).astype(np.float32)]
    return tables


def halves(array):
    high = array.astype(BF16)
    return high, (array - high.astype(F32)).astype(BF16)


def dot(left, right):
    return jnp.dot(left, right, preferred_element_type=F32)


def to_blocks(signal, chips):
    turned = signal.T
    left = turned[:, :LANES].reshape(chips, GROUP, LANES)
    right = turned[:, LANES:].reshape(chips, GROUP, LANES)
    return jnp.concatenate([left, right], axis=1).astype(BF16)


def far_first(count):
    middle = count // 2
    return sorted(range(count), key=lambda step: (abs(step - middle), step))


def kernel(
    chips, columns,
    query_hbm, key_hbm, value_hbm, filt_hbm, cotangent_hbm, input_hbm, weight_hbm,
    one_hbm, two_hi_hbm, two_lo_hbm, inv_hi_hbm, inv_lo_hbm, back_hi_hbm, back_lo_hbm, cos_hbm, sin_hbm,
    skip, suffix_start,
    input_grad, attribution,
    query, key_proj, value, filt, cotangent, layer_input, other_input, own_weight, other_weight,
    one, two_hi, two_lo, inv_hi, inv_lo, back_hi, back_lo, turn_cos, turn_sin,
    send, recv, rows_f32, flat, spec_hi, spec_lo, spec, time_hi, time_lo, results, swapped, outgoing, returned,
    grads, gathered, partial, arrived, totals, others, scores,
    load_sem, send_sem, recv_sem, pair_sem, send_back_sem, recv_back_sem, pair_back_sem,
    share_sem, line_send_sem, line_recv_sem, ring_send_sem, ring_recv_sem, core_sem,
    input_sem,
    gather_send_sem, gather_recv_sem, hand_send_sem, hand_recv_sem, part_send_sem, part_recv_sem, score_send_sem, score_recv_sem,
):
    sources = 2 * chips
    line = min(LINE, chips)
    rings = chips // line
    peers = 2 * columns
    tokens, width = query.shape
    me, lane = lax.axis_index("seq"), lax.axis_index("ch")
    chip, core = me // 2, lax.rem(me, 2)
    y, z = chip // line, lax.rem(chip, line)
    column, side = lane // 2, lax.rem(lane, 2)

    def seat(dy, dz):
        return lax.rem(y + dy + rings, rings) * line + lax.rem(z + dz + line, line)

    def same_core(dy, dz):
        return {"seq": 2 * seat(dy, dz) + core}

    other_core = {"seq": 2 * chip + (1 - core)}
    other_side = {"ch": 2 * column + (1 - side)}

    def along_x(step):
        return {"ch": 2 * lax.rem(column + step + columns, columns) + side}

    def along_ch(step):
        return {"ch": lax.rem(lane + step + peers, peers)}

    barrier = pltpu.get_barrier_semaphore()

    def over_chips(body):
        for dz in far_first(line):
            def one_step(dy, carry, dz=dz):
                body(dy, dz)
                return carry

            lax.fori_loop(1 if dz == 0 else 0, rings, one_step, 0)

    def greet(device):
        pl.semaphore_signal(barrier, inc=1, device_id=device, device_id_type=MESH)

    loads = [
        (key_hbm, key_proj), (value_hbm, value), (filt_hbm, filt), (cotangent_hbm, cotangent), (query_hbm, query),
        (one_hbm, one), (cos_hbm, turn_cos), (sin_hbm, turn_sin), (two_hi_hbm, two_hi), (two_lo_hbm, two_lo),
        (inv_hi_hbm, inv_hi), (inv_lo_hbm, inv_lo), (back_hi_hbm, back_hi), (back_lo_hbm, back_lo),
        (input_hbm, layer_input),
    ]
    loads += [(weight_hbm.at[:, 2 * index + side], own_weight.at[index]) for index in range(columns)]
    loads = [pltpu.make_async_copy(a, b, load_sem.at[i]) for i, (a, b) in enumerate(loads)]
    for load in loads[:5]:
        load.start()
    for step in range(1, peers):
        greet(along_ch(step))
    over_chips(lambda dy, dz: greet(same_core(dy, dz)))
    greet(other_core)
    for load in loads[5:]:
        load.start()

    loads[0].wait()
    loads[1].wait()
    send[:, 0:16, :] = to_blocks(key_proj[...].astype(F32) * value[...].astype(F32), chips)
    loads[2].wait()
    send[:, 16:32, :] = to_blocks(filt[...], chips)
    loads[3].wait()
    loads[4].wait()
    positions = me * tokens + lax.broadcasted_iota(jnp.int32, (tokens, width), 0)
    grad_out = jnp.where(positions >= suffix_start[0], cotangent[...].astype(F32), 0.0)
    send[:, 32:48, :] = to_blocks(grad_out * query[...].astype(F32), chips)

    pl.semaphore_wait(barrier, chips + peers - 1)

    quiet = EARLIEST // (2 * tokens)
    is_quiet = chip < quiet
    rest = chips - quiet

    def forward(dy, dz, short):
        rows = pl.ds(0, 32 if short else 48)
        return pltpu.make_async_remote_copy(
            src_ref=send.at[seat(dy, dz), rows],
            dst_ref=recv.at[core, chip, rows],
            send_sem=send_sem.at[0],
            recv_sem=recv_sem.at[int(short)],
            device_id=same_core(dy, dz),
            device_id_type=MESH,
        )

    def send_signals():
        if quiet:
            @pl.when(is_quiet)
            def _():
                over_chips(lambda dy, dz: forward(dy, dz, True).start())

        @pl.when(jnp.logical_not(is_quiet))
        def _():
            over_chips(lambda dy, dz: forward(dy, dz, False).start())

    def drain(place, semaphore):
        pltpu.make_async_copy(place, place, semaphore).wait()

    def receive_signals(full, short):
        if full:
            drain(recv.at[core, pl.ds(0, full)], recv_sem.at[0])
        if short:
            drain(recv.at[core, pl.ds(0, short), pl.ds(0, 32)], recv_sem.at[1])

    def end_signals():
        if quiet:
            @pl.when(is_quiet)
            def _():
                receive_signals(rest, quiet - 1)

        @pl.when(jnp.logical_not(is_quiet))
        def _():
            receive_signals(rest - 1, quiet)

    def end_sends():
        if quiet and chips > 1:
            @pl.when(is_quiet)
            def _():
                drain(send.at[pl.ds(0, chips - 1), pl.ds(0, 32)], send_sem.at[0])

        @pl.when(jnp.logical_not(is_quiet))
        def _():
            if chips > 1:
                drain(send.at[pl.ds(0, chips - 1)], send_sem.at[0])

    per_column = sources // columns
    share_rows = width // per_column
    share = core * chips + chip
    share_column = share // per_column

    def rows_at(index, count):
        return pl.ds(pl.multiple_of(lax.rem(index, per_column) * share_rows, share_rows), count * share_rows)

    give_share = pltpu.make_async_remote_copy(
        src_ref=weight_hbm.at[:, 2 * share_column + (1 - side), rows_at(share, 1)],
        dst_ref=other_weight.at[share_column, :, rows_at(share, 1)],
        send_sem=share_sem.at[0],
        recv_sem=share_sem.at[1],
        device_id=other_side,
        device_id_type=MESH,
    )
    give_share.start()
    send_signals()
    if quiet:
        recv[core, 0:quiet, 32:48, :] = jnp.zeros((quiet, 16, LANES), BF16)
    recv[core, chip] = send[chip]

    def mirror(index, distance):
        return index + distance * (1 - 2 * lax.rem(index // distance, 2))

    def along_line(step, block, owner):
        place = other_weight.at[share_column, :, rows_at(core * chips + y * line + (mirror(owner) if block else owner), 1)]
        target = mirror(z) if step == 0 else ahead(step)
        return pltpu.make_async_remote_copy(
            src_ref=place,
            dst_ref=place,
            send_sem=line_send_sem.at[2 * step + block],
            recv_sem=line_recv_sem.at[2 * step + block],
            device_id=same_core(0, target - z),
            device_id_type=MESH,
        )

    half_line = line // 2
    within = [(step, block) for step in range(1, half_line) for block in range(2)]

    def mirror(index):
        return index + half_line * (1 - 2 * (index // half_line))

    def ahead(step):
        return z // half_line * half_line + lax.rem(z + step + half_line, half_line)

    end_signals()
    give_share.wait_recv()
    if half_line:
        along_line(0, 0, z).start()

    theirs = pl.ds(pl.multiple_of(16 * (1 - core), 16), 32)
    swap = pltpu.make_async_remote_copy(
        src_ref=recv.at[core, :, theirs],
        dst_ref=recv.at[core, :, theirs],
        send_sem=pair_sem.at[0],
        recv_sem=pair_sem.at[1],
        device_id=other_core,
        device_id_type=MESH,
    )
    swap.start()

    swap.wait_recv()

    def lend_input():
        place = pl.ds(LANES, LANES)
        return pltpu.make_async_remote_copy(
            src_ref=input_hbm.at[place],
            dst_ref=other_input,
            send_sem=input_sem.at[0],
            recv_sem=input_sem.at[1],
            device_id=other_side,
            device_id_type=MESH,
        )

    for index in range(5, 14):
        loads[index].wait()
    sign = jnp.where(core == 0, 1.0, -1.0).astype(F32)
    for signal in range(2):
        if signal == 0:
            rows = recv[:, :, 16:32, :]
        else:
            rows = recv[:, :, pl.ds(pl.multiple_of(32 * core, 16), 16), :]
        rows_f32[...] = rows.astype(F32).reshape(sources * 16, LANES)
        for r in range(16):
            block = rows_f32[pl.ds(r, sources, stride=16), :].astype(BF16)
            flat[:sources, r * LANES : (r + 1) * LANES] = block
            flat[sources:, r * LANES : (r + 1) * LANES] = block
        stage = dot(one[...], flat[...])
        for r in range(16):
            half, channel = r // GROUP, r % GROUP
            span = slice(half * LANES, (half + 1) * LANES)
            real = stage[:sources, r * LANES : (r + 1) * LANES]
            imag = stage[sources:, r * LANES : (r + 1) * LANES]
            cos, sin = turn_cos[:, span], turn_sin[:, span]
            place = slice((signal * GROUP + channel) * sources, (signal * GROUP + channel + 1) * sources)
            spec_hi[place, span], spec_lo[place, span] = halves(real * cos + imag * sin)
            span = slice(tokens + half * LANES, tokens + (half + 1) * LANES)
            spec_hi[place, span], spec_lo[place, span] = halves(imag * cos - real * sin)
    if half_line:
        along_line(0, 0, mirror(z)).wait_recv()
    for step, block in within:
        along_line(step, block, z).start()
    spec[...] = (
        dot(spec_hi[...], two_hi[...]) + dot(spec_lo[...], two_hi[...]) + dot(spec_hi[...], two_lo[...])
    )
    count = GROUP * sources
    fr, fi = spec[:count, :tokens], spec[:count, tokens:] * sign
    pr, pi = spec[count:, :tokens], spec[count:, tokens:]
    product = jnp.concatenate([fr * pr - fi * pi, fr * pi + fi * pr], axis=1)
    prod_hi, prod_lo = halves(product)
    inverse = dot(prod_hi, inv_hi[...]) + dot(prod_lo, inv_hi[...]) + dot(prod_hi, inv_lo[...])
    for r in range(16):
        half, channel = r // GROUP, r % GROUP
        span = slice(half * LANES, (half + 1) * LANES)
        place = slice(channel * sources, (channel + 1) * sources)
        real = inverse[place, span]
        imag = inverse[place, tokens + half * LANES : tokens + (half + 1) * LANES]
        cos, sin = turn_cos[:, span], turn_sin[:, span]
        span = slice(r * LANES, (r + 1) * LANES)
        time_hi[:sources, span], time_lo[:sources, span] = halves(real * cos - imag * sin)
        time_hi[sources:, span], time_lo[sources:, span] = halves(imag * cos + real * sin)
    result = dot(back_hi[...], time_hi[...]) + dot(back_lo[...], time_hi[...]) + dot(back_hi[...], time_lo[...])
    for r in range(16):
        rows_f32[pl.ds(r, sources, stride=16), :] = result[:, r * LANES : (r + 1) * LANES]
    results[...] = rows_f32[...].reshape(2, chips, 16, LANES).astype(BF16)

    swap_back = pltpu.make_async_remote_copy(
        src_ref=results.at[1 - core],
        dst_ref=swapped,
        send_sem=pair_back_sem.at[0],
        recv_sem=pair_back_sem.at[1],
        device_id=other_core,
        device_id_type=MESH,
    )
    swap_back.start()

    def along_ring(step, index):
        first = core * chips + index * line
        place = other_weight.at[first // per_column, :, rows_at(first, line)]
        return pltpu.make_async_remote_copy(
            src_ref=place,
            dst_ref=place,
            send_sem=ring_send_sem.at[step],
            recv_sem=ring_recv_sem.at[step],
            device_id=same_core(step, 0),
            device_id_type=MESH,
        )

    mine = results[core].astype(F32)
    swap_back.wait_recv()
    given = swapped[...].astype(F32)
    conv = jnp.where(core == 0, mine, given)
    corr = jnp.where(core == 0, given, mine)
    for half in range(2):
        span = slice(half * GROUP, (half + 1) * GROUP)
        outgoing[half] = jnp.concatenate([conv[:, span], corr[:, span]], axis=1).astype(BF16)

    def backward(half, dy, dz):
        return pltpu.make_async_remote_copy(
            src_ref=outgoing.at[half, seat(dy, dz)],
            dst_ref=returned.at[half, chip],
            send_sem=send_back_sem.at[half],
            recv_sem=recv_back_sem.at[half],
            device_id=same_core(dy, dz),
            device_id_type=MESH,
        )

    for half in range(2):
        over_chips(lambda dy, dz: backward(half, dy, dz).start())
        returned[half, chip] = outgoing[half, chip]

    for step, block in within:
        along_line(step, block, ahead(-step)).wait_recv()
    for step in range(1, rings):
        along_ring(step, y).start()
    end_sends()
    give_share.wait_send()
    swap.wait_send()
    swap_back.wait_send()
    if half_line:
        along_line(0, 0, z).wait_send()
    for step, block in within:
        along_line(step, block, z).wait_send()

    def gather(part, step):
        return pltpu.make_async_remote_copy(
            src_ref=grads.at[part],
            dst_ref=gathered.at[part, step],
            send_sem=gather_send_sem.at[part, step],
            recv_sem=gather_recv_sem.at[part, step],
            device_id=along_x(-step),
            device_id_type=MESH,
        )

    relayed = columns == 4
    near = (1, 3) if relayed else tuple(range(1, columns))

    def hand_on(part, source):
        span = pl.ds(PART // 2, PART // 2) if source == 1 else pl.ds(0, PART // 2)
        return pltpu.make_async_remote_copy(
            src_ref=gathered.at[part, source, span],
            dst_ref=gathered.at[part, 2, span],
            send_sem=hand_send_sem.at[part, source // 2],
            recv_sem=hand_recv_sem.at[part, source // 2],
            device_id=along_x(-source),
            device_id_type=MESH,
        )

    def end_near(half):
        for part in parts_of(half):
            for step in near:
                gather(part, step).wait_recv()
                if relayed:
                    hand_on(part, step).start()

    def parts_of(half):
        return range(half * LANES // PART, (half + 1) * LANES // PART)

    gains = skip[...]
    for half in range(2):
        if chips > 1:
            drain(returned.at[half, pl.ds(0, chips - 1)], recv_back_sem.at[half])
        if half:
            end_near(0)
        span = slice(half * LANES, (half + 1) * LANES)
        blocks = returned[half].astype(F32)
        conv_out = blocks[:, :GROUP].reshape(width, LANES).T
        corr_out = blocks[:, GROUP:].reshape(width, LANES).T
        keys = key_proj[span, :].astype(F32)
        values = value[span, :].astype(F32)
        positions = me * tokens + half * LANES + lax.broadcasted_iota(jnp.int32, (LANES, width), 0)
        grad_out = jnp.where(positions >= suffix_start[0], cotangent[span, :].astype(F32), 0.0)
        grad_mixed = corr_out + gains * (grad_out * query[span, :].astype(F32))
        pieces = (grad_out * (conv_out + gains * (keys * values)), grad_mixed * values, grad_mixed * keys)
        pieces = jnp.concatenate(pieces, axis=1).astype(BF16)
        for index, part in enumerate(parts_of(half)):
            grads[part] = pieces[index * PART : (index + 1) * PART]
            for step in near:
                gather(part, step).start()
    lend_input().start()

    for step in range(1, rings):
        along_ring(step, lax.rem(y - step + rings, rings)).wait_recv()
    portion = other_weight.at[pl.ds(core * (columns // 2), columns // 2)]
    give_core = pltpu.make_async_remote_copy(
        src_ref=portion,
        dst_ref=portion,
        send_sem=core_sem.at[0],
        recv_sem=core_sem.at[1],
        device_id=other_core,
        device_id_type=MESH,
    )
    give_core.start()

    def exchange(part):
        return pltpu.make_async_remote_copy(
            src_ref=partial.at[part],
            dst_ref=arrived.at[part],
            send_sem=part_send_sem.at[part],
            recv_sem=part_recv_sem.at[part],
            device_id=other_side,
            device_id_type=MESH,
        )

    def weight_at(step, weight):
        return weight[lax.rem(column + step, columns)].reshape(3 * width, -1)

    for half in range(2):
        if half:
            end_near(half)
        else:
            give_core.wait_recv()
        rows = slice(parts_of(half)[0], parts_of(half)[-1] + 1)
        other = dot(grads[rows].reshape(LANES, -1), weight_at(0, other_weight))
        for step in near:
            if half == 0 and not relayed:
                for part in parts_of(half):
                    gather(part, step).wait_recv()
            other += dot(gathered[rows, step].reshape(LANES, -1), weight_at(step, other_weight))
        others[half] = other
        for index, part in enumerate(parts_of(half)):
            span = slice(index * PART, (index + 1) * PART)
            if relayed:
                hand_on(part, 1).wait_recv()
                hand_on(part, 3).wait_recv()
                others[half, span] += dot(gathered[part, 2], weight_at(2, other_weight))
            partial[part] = others[half, span].astype(BF16)
            exchange(part).start()

    for index in range(14, len(loads)):
        loads[index].wait()
    for half in range(2):
        rows = slice(parts_of(half)[0], parts_of(half)[-1] + 1)
        own = dot(grads[rows].reshape(LANES, -1), weight_at(0, own_weight))
        for step in range(1, columns):
            own += dot(gathered[rows, step].reshape(LANES, -1), weight_at(step, own_weight))
        totals[half] = own

    def tell(half, step, index):
        return pltpu.make_async_remote_copy(
            src_ref=scores.at[index, half],
            dst_ref=scores.at[index, half],
            send_sem=score_send_sem.at[half, step],
            recv_sem=score_recv_sem.at[half, step],
            device_id=along_ch(step),
            device_id_type=MESH,
        )

    def share_scores(half, weighted):
        features = weighted.shape[1]
        folded = weighted[:, : min(LANES, features)]
        for start in range(LANES, features, LANES):
            folded = folded + weighted[:, start : start + LANES]
        scores[lane, half] = jnp.broadcast_to(jnp.sum(folded.T, axis=0, keepdims=True), (8, LANES))
        for step in range(1, peers):
            tell(half, step, lane).start()

    def finish(half):
        for part in parts_of(half):
            exchange(part).wait_recv()
        rows = slice(parts_of(half)[0], parts_of(half)[-1] + 1)
        full_grad = totals[half] + arrived[rows].astype(F32).reshape(LANES, -1)
        input_grad[half * LANES : (half + 1) * LANES, :] = full_grad.astype(BF16)
        return full_grad

    give_core.wait_send()
    for step in range(1, rings):
        along_ring(step, y).wait_send()
    for half in range(2):
        if chips > 1:
            drain(outgoing.at[half, pl.ds(0, chips - 1)], send_back_sem.at[half])
        for part in parts_of(half):
            for step in near:
                gather(part, step).wait_send()
                if relayed:
                    hand_on(part, step).wait_send()

    share_scores(0, finish(0) * layer_input[:LANES, :].astype(F32))
    lend_input().wait_recv()
    share_scores(
        1, totals[1] * layer_input[LANES:, :].astype(F32) + others[1] * other_input[...].astype(F32)
    )
    finish(1)
    lend_input().wait_send()
    for part in range(tokens // PART):
        exchange(part).wait_send()

    for half in range(2):
        for step in range(1, peers):
            tell(half, step, lax.rem(lane - step + peers, peers)).wait_recv()
        total = scores[0, half]
        for index in range(1, peers):
            total = total + scores[index, half]
        attribution[:, half * LANES : (half + 1) * LANES] = total[0:1, :]
    for half in range(2):
        for step in range(1, peers):
            tell(half, step, lane).wait_send()


def shards(query, key_proj, value, filt, skip, cotangent, suffix_start, layer_input, in_weight):
    tokens, width = query.shape
    features = in_weight.shape[1]
    sources, peers = lax.axis_size("seq"), lax.axis_size("ch")
    chips, columns = sources // 2, peers // 2
    line = min(LINE, chips)
    rings = chips // line
    tables = transform_tables(sources, tokens)
    count = GROUP * sources
    parts = tokens // PART
    vmem = pl.BlockSpec(memory_space=pltpu.VMEM)
    smem = pl.BlockSpec(memory_space=pltpu.SMEM)
    hbm = pl.BlockSpec(memory_space=pl.ANY)
    dma = pltpu.SemaphoreType.DMA
    block = pltpu.VMEM((tokens, width), BF16)
    weight_block = pltpu.VMEM((columns, 3, width, features), BF16)
    input_grad, attribution = pl.pallas_call(
        functools.partial(kernel, chips, columns),
        out_shape=(jax.ShapeDtypeStruct((tokens, features), BF16), jax.ShapeDtypeStruct((1, tokens), F32)),
        in_specs=[hbm] * (7 + len(tables)) + [vmem, smem],
        out_specs=(vmem, vmem),
        scratch_shapes=[
            block, block, block, pltpu.VMEM((tokens, width), F32), block,
            pltpu.VMEM((tokens, features), BF16), pltpu.VMEM((LANES, features), BF16),
            weight_block, weight_block,
            *[pltpu.VMEM(table.shape, table.dtype) for table in tables],
            pltpu.VMEM((chips, 48, LANES), BF16),
            pltpu.VMEM((2, chips, 48, LANES), BF16),
            pltpu.VMEM((sources * 16, LANES), F32),
            pltpu.VMEM((2 * sources, 16 * LANES), BF16),
            pltpu.VMEM((2 * count, 2 * tokens), BF16),
            pltpu.VMEM((2 * count, 2 * tokens), BF16),
            pltpu.VMEM((2 * count, 2 * tokens), F32),
            pltpu.VMEM((2 * sources, 16 * LANES), BF16),
            pltpu.VMEM((2 * sources, 16 * LANES), BF16),
            pltpu.VMEM((2, chips, 16, LANES), BF16),
            pltpu.VMEM((chips, 16, LANES), BF16),
            pltpu.VMEM((2, chips, 16, LANES), BF16),
            pltpu.VMEM((2, chips, 16, LANES), BF16),
            pltpu.VMEM((parts, PART, 3 * width), BF16),
            pltpu.VMEM((parts, columns, PART, 3 * width), BF16),
            pltpu.VMEM((parts, PART, features), BF16),
            pltpu.VMEM((parts, PART, features), BF16),
            pltpu.VMEM((2, LANES, features), F32),
            pltpu.VMEM((2, LANES, features), F32),
            pltpu.VMEM((peers, 2, 8, LANES), F32),
            dma((15 + columns,)),
            dma((1,)), dma((2,)), dma((2,)),
            dma((2,)), dma((2,)), dma((2,)),
            dma((2,)), dma((line,)), dma((line,)), dma((rings,)), dma((rings,)), dma((2,)),
            dma((2,)),
            dma((parts, columns)), dma((parts, columns)), dma((parts, 2)), dma((parts, 2)),
            dma((parts,)), dma((parts,)), dma((2, peers)), dma((2, peers)),
        ],
        compiler_params=pltpu.CompilerParams(
            collective_id=0, has_side_effects=True, vmem_limit_bytes=56 * 1024 * 1024
        ),
        name="conv_backward",
    )(
        query, key_proj, value, filt, cotangent, layer_input, in_weight.reshape(3, peers, width, features),
        *[jnp.asarray(table) for table in tables],
        skip[None, :], suffix_start,
    )
    return input_grad, attribution[0]


def solution(mesh):
    in_specs = (
        P("seq", "ch"),
        P("seq", "ch"),
        P("seq", "ch"),
        P("seq", "ch"),
        P("ch"),
        P("seq", "ch"),
        P(),
        P("seq", "ch"),
        P(None, "ch"),
    )
    out_specs = (P("seq", "ch"), P("seq"))
    return jax.shard_map(shards, mesh=mesh, in_specs=in_specs, out_specs=out_specs, check_vma=False)
```
